256 devices in a mesh: shard: 32 (over z, y), rep: 8 (over x, core).
Axes of the slice: x: 4, y: 4, z: 8, core: 2. Of those that a mesh axis runs over, the one named last changes fastest.
Arguments:
- queries: bfloat16 [1024, 32, 128], P(('shard', 'rep')), may hold values from -1.796875 to 1.796875
- passages: bfloat16 [8192, 72, 128], P('shard'), may hold values from -1.796875 to 1.796875
- cand_rows: int32 [1024, 32, 32], P(('shard', 'rep')), may hold values from 0 to 255
- cand_counts: int32 [1024, 32], P(('shard', 'rep')), may hold values from 0 to 32, as said below
Outputs:
- scores: float32 [1024, 32, 32], P(('shard', 'rep'))
The draws below stay inside these ranges and needn't reach their ends.
Inputs may be any that keep to these rules, and one draw needn't show every extreme that they name: `cand_rows`: slots at or past the count hold rows that are not used. `cand_counts`: some query has 32 live slots in some shard in every draw.
All inputs are finite; a program needn't handle non-finite values.
Results may differ from the reference program's by a relative error of at most 0.0003.
Values may be sent and summed in bfloat16 or wider, within the bound.
A program may use at most 64 MiB of HBM per device.

```python
import jax
import jax.numpy as jnp
from jax import lax

DIM = 128
QTOK = 32
PTOK = 72
PLEN = 70
CAP = 32
P_SHARD = 256
QUERIES = 1024
PASSAGES = 8192
N_SHARD = 32


def draw_cand_counts(key, part):
    key = jax.random.fold_in(key, 7)
    key_heavy, key_first, key_count = jax.random.split(key, 3)
    shard_ids = jnp.arange(N_SHARD)
    chosen = jax.random.randint(key_first, (), 0, N_SHARD)
    heavy = (jax.random.randint(key_heavy, (N_SHARD,), 0, 4) == 0) | (shard_ids == chosen)
    highest = jnp.where(heavy, CAP, max(CAP // 4, 1))
    counts = jax.random.randint(key_count, (QUERIES, N_SHARD), 0, highest[None, :] + 1)
    query_ids = jnp.arange(QUERIES)
    forced = (query_ids[:, None] == 0) & (shard_ids[None, :] == chosen)
    return jnp.where(forced, CAP, counts).astype(jnp.int32)


def touch_ends(result, stream_key, smallest, high):
    longest = result.shape.index(max(result.shape))
    spots = []
    for shift in (0, 1):
        where = [jax.random.randint(jax.random.fold_in(stream_key, axis), (), 0, length) for axis, length in enumerate(result.shape)]
        where[longest] = (where[longest] + shift) % result.shape[longest]
        spots.append(tuple(where))
    return result.at[spots[0]].set(smallest).at[spots[1]].set(high)


def block_scale(rng, shape, pieces, low, high):
    gain, own = 1.0, jax.random.fold_in(rng, 6)
    for axis_at, parts in pieces:
        draws = jnp.exp(jax.random.uniform(jax.random.fold_in(own, axis_at), (parts,), jnp.float32, low / len(pieces), high / len(pieces)))
        gain = gain * jnp.repeat(draws, shape[axis_at] // parts).reshape([-1 if axis == axis_at else 1 for axis in range(len(shape))])
    return gain


def bell_draw(rng, extent, spread, reach, cuts=(), held_as=jnp.bfloat16):
    loudness = block_scale(rng, extent, cuts, -0.22, 0.18) if cuts else 1.0
    values = jax.random.normal(rng, extent, jnp.float32) * spread * loudness
    return jnp.minimum(jnp.maximum(values, -reach), reach).astype(held_as)


def setup_inputs(seed: int = 0) -> dict:
    arg_keys = jax.random.split(jax.random.key(seed), 5)
    queries = bell_draw(arg_keys[0], (QUERIES, QTOK, DIM), 0.3, 1.796875, ((0, 256),))
    passages = bell_draw(arg_keys[1], (PASSAGES, PTOK, DIM), 0.3, 1.796875, ((0, 32),))
    cand_rows = touch_ends(jax.random.randint(arg_keys[2], (QUERIES, N_SHARD, CAP), 0, P_SHARD), jax.random.fold_in(arg_keys[2], 1), 0, P_SHARD - 1).astype(jnp.int32)
    cand_counts = draw_cand_counts(jax.random.fold_in(arg_keys[4], 71), 0)
    return {"queries": queries, "passages": passages, "cand_rows": cand_rows, "cand_counts": cand_counts}


def score_query(query_tok, flat_rows, passages):
    picked = passages[flat_rows].astype(jnp.float32)
    sims = jnp.einsum("td,cpd->ctp", query_tok.astype(jnp.float32), picked)
    valid = jnp.arange(PTOK) < PLEN
    sims = jnp.where(valid[None, None, :], sims, -jnp.inf)
    best = jnp.max(sims, axis=-1)
    return jnp.mean(best, axis=-1)


def reference(queries, passages, cand_rows, cand_counts):
    offsets = (jnp.arange(N_SHARD) * P_SHARD).astype(jnp.int32)
    global_rows = (cand_rows + offsets[None, :, None]).astype(jnp.int32)
    flat = global_rows.reshape(QUERIES, N_SHARD * CAP)
    values = lax.map(lambda pair: score_query(pair[0], pair[1], passages), (queries, flat))
    values = values.reshape(QUERIES, N_SHARD, CAP)
    slots = jnp.arange(CAP).astype(jnp.int32)
    live = slots[None, None, :] < cand_counts[:, :, None]
    return jnp.where(live, values, jnp.float32(0.0))
```

```python
import functools

import jax
import jax.numpy as jnp
from jax import lax
from jax.experimental import pallas as pl
from jax.experimental.pallas import tpu as pltpu
from jax.sharding import PartitionSpec as P

PLEN = 70
PTOK = 72
NZ = 8
NY = 4
N = NZ * NY
CAP = 32
QTOK = 32
GROUP = 16
Y_ORDER = (0, 1, 3, 2)
MESH = pl.DeviceIdType.MESH


def partner(me, i, dy, sign):
    dz = ((i + 1) // 2) * (2 * (i % 2) - 1)
    z, y = me // NY, me % NY
    return ((z + sign * dz + NZ) % NZ) * NY + (y + sign * dy + NY) % NY


def score_block(query_block, rows, block, passages):
    token = lax.broadcasted_iota(jnp.int32, (8, 128), 0)
    best = []
    for first in range(0, 128, GROUP):
        picked = [passages[rows[block, 0, first + k] & 255] for k in range(GROUP)]
        sims = lax.dot_general(
            jnp.concatenate(picked, 0), query_block, (((1,), (1,)), ((), ())), preferred_element_type=jnp.float32
        ).reshape(GROUP, PTOK // 8, 8, 128)
        head = jnp.max(sims[:, : PTOK // 8 - 1], axis=1)
        tail = jnp.where(token[None] < PLEN - (PTOK - 8), sims[:, PTOK // 8 - 1], -jnp.inf)
        best.append(jnp.max(jnp.maximum(head, tail), axis=1))
    best = jnp.concatenate(best, 0)
    slot = lax.broadcasted_iota(jnp.int32, (128, 128), 0)
    lane = lax.broadcasted_iota(jnp.int32, (128, 128), 1)
    own = jnp.where(slot // CAP == lane // QTOK, best, 0.0)
    mean = jnp.sum(own, axis=1, keepdims=True) * (1.0 / QTOK)
    return jnp.sum(jnp.where(slot == lane, mean, 0.0), axis=0, keepdims=True)


def kernel(queries, passages, cand_rows, cand_counts, out, held, corpus, rows_out, rows_in, rows_s, score_out, score_in,
           load_sem, q_send, q_recv, r_send, r_recv, s_send, s_recv, own_sem):
    me = lax.axis_index("shard")

    def q_copy(k, to, slot):
        return pltpu.make_async_remote_copy(
            src_ref=queries, dst_ref=held.at[slot], send_sem=q_send.at[k], recv_sem=q_recv.at[k],
            device_id={"shard": to}, device_id_type=MESH)

    def r_copy(k, to):
        return pltpu.make_async_remote_copy(
            src_ref=rows_out.at[to], dst_ref=rows_in.at[k], send_sem=r_send.at[k], recv_sem=r_recv.at[k],
            device_id={"shard": to}, device_id_type=MESH)

    def s_copy(k, to):
        return pltpu.make_async_remote_copy(
            src_ref=score_out.at[k], dst_ref=score_in.at[me], send_sem=s_send.at[k], recv_sem=s_recv.at[k],
            device_id={"shard": to}, device_id_type=MESH)

    loads = []
    quarter = passages.shape[0] // 4
    for part in range(4):
        span = pl.ds(part * quarter, quarter)
        loads.append(pltpu.make_async_copy(passages.at[span], corpus.at[span], load_sem.at[part]))
        loads[-1].start()

    barrier = pltpu.get_barrier_semaphore()
    for i in range(NZ):
        for j, dy in enumerate(Y_ORDER):
            if i or j:
                pl.semaphore_signal(barrier, inc=1, device_id={"shard": partner(me, i, dy, 1)}, device_id_type=MESH)
    packed = jnp.concatenate([cand_rows[q] for q in range(4)], axis=1)
    for s in range(N):
        rows_out[s] = packed[s : s + 1]
    own_rows = pltpu.make_async_copy(rows_out.at[me], rows_in.at[0], own_sem.at[0])
    own_rows.start()
    own_queries = pltpu.make_async_copy(queries, held.at[0], own_sem.at[1])
    own_queries.start()
    pl.semaphore_wait(barrier, N - 1)

    for i in range(NZ):
        for j, dy in enumerate(Y_ORDER):
            if i or j:
                r_copy(i * NY + j, partner(me, i, dy, 1)).start()
    for i in range(NZ):
        for j, dy in enumerate(Y_ORDER):
            if i or j:
                k = i * NY + j
                q_copy(k, partner(me, i, dy, 1), k).start()

    own_rows.wait()
    own_queries.wait()
    for k in range(1, N):
        r_copy(k, me).wait_recv()
    to_smem = pltpu.make_async_copy(rows_in, rows_s, own_sem.at[2])
    to_smem.start()
    for load in loads:
        load.wait()
    to_smem.wait()

    def step(i, _):
        for j, dy in enumerate(Y_ORDER):
            k = i * NY + j

            @pl.when(k > 0)
            def _():
                q_copy(k, me, k).wait_recv()

        for j, dy in enumerate(Y_ORDER):
            k = i * NY + j
            score_out[k] = score_block(held[k], rows_s, k, corpus)
        for j, dy in enumerate(Y_ORDER):
            k = i * NY + j

            @pl.when(k > 0)
            def _():
                s_copy(k, partner(me, i, dy, -1)).start()

        return 0

    lax.fori_loop(0, NZ, step, 0)
    own_score = pltpu.make_async_copy(score_out.at[0], score_in.at[me], own_sem.at[3])
    own_score.start()
    own_score.wait()
    for k in range(1, N):
        q_copy(k, me, k).wait_send()
        r_copy(k, me).wait_send()
        s_copy(k, me).wait_send()
        s_copy(k, me).wait_recv()
    returned = score_in[...].reshape(N, 128)
    slot = lax.broadcasted_iota(jnp.int32, (N, CAP), 1)
    for q in range(4):
        live = slot < cand_counts[q : q + 1, :].reshape(N, 1)
        out[q] = jnp.where(live, returned[:, q * CAP : (q + 1) * CAP], 0.0)


def body(queries, passages, cand_rows, cand_counts):
    count = queries.shape[0]
    block = queries.reshape(count * QTOK, queries.shape[2])
    vmem = pl.BlockSpec(memory_space=pltpu.VMEM)
    dma = pltpu.SemaphoreType.DMA
    return pl.pallas_call(
        kernel,
        out_shape=jax.ShapeDtypeStruct((count, N, CAP), jnp.float32),
        in_specs=[vmem, pl.BlockSpec(memory_space=pl.ANY), vmem, vmem],
        out_specs=vmem,
        scratch_shapes=[
            pltpu.VMEM((N,) + block.shape, jnp.bfloat16),
            pltpu.VMEM(passages.shape, jnp.bfloat16),
            pltpu.VMEM((N, 1, 128), jnp.int32),
            pltpu.VMEM((N, 1, 128), jnp.int32),
            pltpu.SMEM((N, 1, 128), jnp.int32),
            pltpu.VMEM((N, 1, 128), jnp.float32),
            pltpu.VMEM((N, 1, 128), jnp.float32),
            dma((4,)),
            dma((N,)), dma((N,)), dma((N,)), dma((N,)), dma((N,)), dma((N,)),
            dma((4,)),
        ],
        compiler_params=pltpu.CompilerParams(collective_id=0, has_side_effects=True, vmem_limit_bytes=32 << 20),
        cost_estimate=pl.CostEstimate(flops=2 * 4096 * 72 * 32 * 128, bytes_accessed=6 << 20, transcendentals=0),
        name="maxsim",
    )(block, passages, cand_rows, cand_counts)


def solution(mesh):
    return jax.shard_map(
        body,
        mesh=mesh,
        in_specs=(
            P(("shard", "rep"), None, None),
            P("shard", None, None),
            P(("shard", "rep"), None, None),
            P(("shard", "rep"), None),
        ),
        out_specs=P(("shard", "rep"), None, None),
        check_vma=False,
    )
```

```python
import jax
import jax.numpy as jnp
from jax import lax
from jax.experimental import pallas as pl
from jax.experimental.pallas import tpu as pltpu
from jax.sharding import PartitionSpec as P

PLEN = 70
PTOK = 72
NZ = 8
NY = 4
HALF = NZ // 2
N = NZ * NY
CAP = 32
QTOK = 32
LANES = 128
GROUP = 16
MESH = pl.DeviceIdType.MESH


def plane(i, z):
    near = (z + i) % HALF
    if_low = jnp.where(i < HALF, near, HALF + near)
    if_high = jnp.where((i < 2) | (i >= 2 + HALF), HALF + near, i - 2)
    return jnp.where(z < HALF, if_low, if_high)


def score_block(query_block, row_at, passages):
    token = lax.broadcasted_iota(jnp.int32, (8, LANES), 0)
    best = []
    for first in range(0, LANES, GROUP):
        picked = [passages[row_at(first + k) & 255] for k in range(GROUP)]
        sims = lax.dot_general(
            jnp.concatenate(picked, 0), query_block, (((1,), (1,)), ((), ())), preferred_element_type=jnp.float32
        ).reshape(GROUP, PTOK // 8, 8, LANES)
        head = jnp.max(sims[:, : PTOK // 8 - 1], axis=1)
        tail = jnp.where(token[None] < PLEN - (PTOK - 8), sims[:, PTOK // 8 - 1], -jnp.inf)
        best.append(jnp.max(jnp.maximum(head, tail), axis=1))
    best = jnp.concatenate(best, 0)
    slot = lax.broadcasted_iota(jnp.int32, (LANES, LANES), 0)
    lane = lax.broadcasted_iota(jnp.int32, (LANES, LANES), 1)
    own = jnp.where(slot // CAP == lane // QTOK, best, 0.0)
    mean = jnp.sum(own, axis=1, keepdims=True) * (1.0 / QTOK)
    return jnp.sum(jnp.where(slot == lane, mean, 0.0), axis=0, keepdims=True)


def kernel(queries, passages, cand_rows, cand_counts, out, held, corpus, rows_v, rows_s, score_out, score_in,
           own_rows, own_counts, load_sem, in_sem, rows_sem, q_send, q_recv, s_send, s_recv, ready_z, ready_y):
    me = lax.axis_index("shard")
    z, y = me // NY, me % NY

    def send_block(s, to):
        pltpu.make_async_remote_copy(
            src_ref=held.at[s], dst_ref=held.at[s], send_sem=q_send, recv_sem=q_recv.at[s],
            device_id={"shard": to}, device_id_type=MESH).start()

    def wait_block(s):
        pltpu.make_async_copy(held.at[s], held.at[s], q_recv.at[s]).wait()

    def send_score(s):
        @pl.when(s != me)
        def _():
            pltpu.make_async_remote_copy(
                src_ref=score_out.at[s], dst_ref=score_in.at[me], send_sem=s_send, recv_sem=s_recv,
                device_id={"shard": s}, device_id_type=MESH).start()

    def spread(i):
        s = plane(i, z) * NY + y
        wait_block(s)
        for dy in range(1, NY):
            send_block(s, z * NY + (y + dy) % NY)

    def unpack_rows(i):
        mine = lax.broadcasted_iota(jnp.int32, (N, LANES), 0) == me
        for j in range(NY):
            rows = held[plane(i, z) * NY + j, 4 * QTOK :].astype(jnp.float32)
            rows_v[i, j : j + 1] = jnp.sum(jnp.where(mine, rows, 0.0), axis=0, keepdims=True).astype(jnp.int32)
        pltpu.make_async_copy(rows_v.at[i], rows_s.at[i], rows_sem.at[i]).start()

    def collect(i):
        for dy in range(1, NY):
            wait_block(plane(i, z) * NY + (y + dy) % NY)
        unpack_rows(i)

    rows_in = pltpu.make_async_copy(cand_rows, own_rows, in_sem.at[0])
    queries_in = pltpu.make_async_copy(queries, held.at[me, pl.ds(0, 4 * QTOK)], in_sem.at[1])
    counts_in = pltpu.make_async_copy(cand_counts, own_counts, in_sem.at[2])
    rows_in.start()
    queries_in.start()
    counts_in.start()
    loads = []
    part = passages.shape[0] // 4
    for k in range(4):
        span = pl.ds(k * part, part)
        loads.append(pltpu.make_async_copy(passages.at[span], corpus.at[span], load_sem.at[k]))
        loads[-1].start()

    barrier = pltpu.get_barrier_semaphore()
    for d in range(1, NZ):
        to = (z + d) % NZ

        @pl.when(to > z)
        def _():
            pl.semaphore_signal(barrier, inc=1, device_id={"shard": to * NY + y}, device_id_type=MESH)

    for d in range(1, NY):
        to = (y + d) % NY

        @pl.when(to > y)
        def _():
            pl.semaphore_signal(barrier, inc=1, device_id={"shard": z * NY + to}, device_id_type=MESH)

    rows_in.wait()
    packed = jnp.concatenate([own_rows[q] for q in range(4)], axis=1)
    held[me, 4 * QTOK :] = packed.astype(jnp.float32).astype(jnp.bfloat16)
    queries_in.wait()

    @pl.when(me > 0)
    def _():
        pl.semaphore_wait(barrier, z + y)

    for d in range(1, NY):
        to = (y + d) % NY

        @pl.when(to < y)
        def _():
            pl.semaphore_signal(ready_y.at[y], inc=1, device_id={"shard": z * NY + to}, device_id_type=MESH)
            send_block(me, z * NY + to)

    for d in range(1, NZ):
        to = (z + d) % NZ

        @pl.when(to < z)
        def _():
            pl.semaphore_signal(ready_z.at[z], inc=1, device_id={"shard": to * NY + y}, device_id_type=MESH)
            send_block(me, to * NY + y)

    for d in range(1, NY):
        to = y + d

        @pl.when(to < NY)
        def _():
            pl.semaphore_wait(ready_y.at[to], 1)
            send_block(me, z * NY + to)

    def greet_later(first, last):
        for d in range(1, HALF):
            to = z + d

            @pl.when((to >= first) & (to < last))
            def _():
                pl.semaphore_wait(ready_z.at[to], 1)
                send_block(me, to * NY + y)

    greet_later(0, jnp.where(z < HALF, HALF, NZ))
    spread(1)
    collect(0)
    for load in loads:
        load.wait()

    def step(i, _):
        @pl.when((i == 1) & (z < HALF))
        def _():
            for to in range(HALF, NZ):
                pl.semaphore_wait(ready_z.at[to], 1)
                send_block(me, to * NY + y)

        @pl.when(i + 2 < NZ)
        def _():
            spread(i + 2)

        @pl.when(i > 0)
        def _():
            for j in range(NY):
                send_score(plane(i - 1, z) * NY + j)

        @pl.when(i + 1 < NZ)
        def _():
            collect(i + 1)

        pltpu.make_async_copy(rows_v.at[i], rows_s.at[i], rows_sem.at[i]).wait()
        for j in range(NY):
            s = plane(i, z) * NY + j
            score_out[s] = score_block(held[s, : 4 * QTOK], lambda k, j=j: rows_s[i, j, k], corpus)
        return 0

    lax.fori_loop(0, NZ, step, 0)
    for j in range(NY):
        send_score(plane(NZ - 1, z) * NY + j)
    score_in[me] = score_out[me]
    counts_in.wait()
    others = pl.ds(0, N - 1)
    pltpu.make_async_copy(held.at[others], held.at[others], q_send).wait()
    pltpu.make_async_copy(score_in.at[others], score_in.at[others], s_send).wait()
    pltpu.make_async_copy(score_in.at[others], score_in.at[others], s_recv).wait()
    returned = score_in[...].reshape(N, LANES)
    slot = lax.broadcasted_iota(jnp.int32, (N, CAP), 1)
    for q in range(4):
        live = slot < own_counts[q : q + 1, :].reshape(N, 1)
        out[q] = jnp.where(live, returned[:, q * CAP : (q + 1) * CAP], 0.0)


def body(queries, passages, cand_rows, cand_counts):
    count = queries.shape[0]
    block = queries.reshape(count * QTOK, queries.shape[2])
    hbm = pl.BlockSpec(memory_space=pltpu.HBM)
    dma = pltpu.SemaphoreType.DMA
    regular = pltpu.SemaphoreType.REGULAR
    return pl.pallas_call(
        kernel,
        out_shape=jax.ShapeDtypeStruct((count, N, CAP), jnp.float32),
        in_specs=[hbm, hbm, hbm, hbm],
        out_specs=pl.BlockSpec(memory_space=pltpu.VMEM),
        scratch_shapes=[
            pltpu.VMEM((N, block.shape[0] + N, LANES), jnp.bfloat16),
            pltpu.VMEM(passages.shape, jnp.bfloat16),
            pltpu.VMEM((NZ, NY, LANES), jnp.int32),
            pltpu.SMEM((NZ, NY, LANES), jnp.int32),
            pltpu.VMEM((N, 1, LANES), jnp.float32),
            pltpu.VMEM((N, 1, LANES), jnp.float32),
            pltpu.VMEM(cand_rows.shape, jnp.int32),
            pltpu.VMEM(cand_counts.shape, jnp.int32),
            dma((4,)), dma((3,)), dma((NZ,)),
            dma, dma((N,)), dma, dma,
            regular((NZ,)), regular((NY,)),
        ],
        compiler_params=pltpu.CompilerParams(collective_id=0, has_side_effects=True, vmem_limit_bytes=(64 << 20) - (64 << 10)),
        cost_estimate=pl.CostEstimate(flops=2 * 4096 * 72 * 32 * 128, bytes_accessed=6 << 20, transcendentals=0),
        name="maxsim",
    )(block, passages, cand_rows, cand_counts)


def solution(mesh):
    return jax.shard_map(
        body,
        mesh=mesh,
        in_specs=(
            P(("shard", "rep"), None, None),
            P("shard", None, None),
            P(("shard", "rep"), None, None),
            P(("shard", "rep"), None),
        ),
        out_specs=P(("shard", "rep"), None, None),
        check_vma=False,
    )
```

```python
import jax
import jax.numpy as jnp
from jax import lax
from jax.experimental import pallas as pl
from jax.experimental.pallas import tpu as pltpu
from jax.sharding import PartitionSpec as P

PLEN = 70
PTOK = 72
NZ = 8
NY = 4
HALF = NZ // 2
N = NZ * NY
CAP = 32
QTOK = 32
LANES = 128
GROUP = 16
MESH = pl.DeviceIdType.MESH


ORDER = (
    ((0, 0), (0, 3), (1, 3), (0, 2), (1, 2), (0, 1), (1, 0), (1, 1)),
    ((0, 0), (0, 2), (1, 1), (1, 3), (1, 0), (1, 2), (0, 3), (0, 1)),
)
SENDS = (
    {
        -1: (("y", 3), ("o", (0, 3)), ("y", 1), ("y", 2), ("o", (0, 2)), ("o", (1, 3)),),
        0: (("s", 1), ("o", (1, 1)), ("s", 3), ("o", (0, 1)),),
        1: (("o", (1, 2)), ("s", 2), ("o", (1, 0)),),
        2: (("s", 6), ("s", 4),),
        3: (("s", 5),),
        4: (("s", 7),),
    },
    {
        -1: (("y", 3), ("o", (0, 3)), ("y", 1), ("y", 2), ("o", (0, 2)), ("o", (1, 3)),),
        0: (("s", 1), ("o", (1, 1)), ("s", 3), ("o", (0, 1)),),
        1: (("o", (1, 2)), ("s", 2), ("o", (1, 0)),),
        2: (("s", 6), ("s", 4),),
        3: (("s", 5),),
        4: (("s", 7),),
    },
    {
        -1: (("y", 3), ("o", (0, 3)), ("y", 1), ("y", 2), ("o", (0, 2)), ("o", (1, 3)),),
        0: (("s", 1), ("o", (1, 1)), ("s", 3), ("o", (0, 1)),),
        1: (("o", (1, 2)), ("s", 2), ("o", (1, 0)),),
        2: (("s", 6), ("s", 4),),
        3: (("s", 5),),
        4: (("s", 7),),
    },
    {
        -1: (("y", 3), ("o", (0, 3)), ("y", 1), ("y", 2), ("o", (0, 2)), ("o", (1, 3)),),
        0: (("s", 1), ("o", (1, 1)), ("s", 3), ("o", (0, 1)),),
        1: (("o", (1, 2)), ("s", 2), ("o", (1, 0)),),
        2: (("s", 6), ("s", 4),),
        3: (("s", 5),),
        4: (("s", 7),),
    },
    {
        -1: (("y", 1), ("o", (0, 2)), ("y", 3), ("y", 2), ("o", (1, 3)), ("o", (1, 2)), ("s", 1), ("o", (1, 0)),),
        0: (("s", 3),),
        1: (("o", (0, 3)), ("s", 2), ("o", (0, 1)),),
        2: (("o", (1, 1)), ("s", 4), ("s", 5),),
        3: (("s", 6),),
        4: (("s", 7),),
    },
    {
        -1: (("y", 1), ("o", (0, 2)), ("y", 3), ("y", 2), ("o", (1, 3)), ("o", (1, 2)), ("s", 1), ("o", (1, 0)),),
        0: (("s", 3),),
        1: (("o", (0, 3)), ("s", 2), ("o", (0, 1)),),
        2: (("o", (1, 1)), ("s", 4), ("s", 5),),
        3: (("s", 6),),
        4: (("s", 7),),
    },
    {
        -1: (("y", 1), ("o", (0, 2)), ("y", 3), ("y", 2), ("o", (1, 3)), ("o", (1, 2)), ("s", 1), ("o", (1, 0)),),
        0: (("s", 3),),
        1: (("o", (0, 3)), ("s", 2), ("o", (0, 1)),),
        2: (("o", (1, 1)), ("s", 4), ("s", 5),),
        3: (("s", 6),),
        4: (("s", 7),),
    },
    {
        -1: (("y", 1), ("o", (0, 2)), ("y", 3), ("y", 2), ("o", (1, 3)), ("o", (1, 2)), ("s", 1), ("o", (1, 0)),),
        0: (("s", 3),),
        1: (("o", (0, 3)), ("s", 2), ("o", (0, 1)),),
        2: (("o", (1, 1)), ("s", 4), ("s", 5),),
        3: (("s", 6),),
        4: (("s", 7),),
    },
)
ROWS_AT = (
    (-1, 1, 2, 2, 4, 5, 5, 6),
    (-1, 1, 2, 2, 3, 4, 5, 6),
)


def apart(a, b):
    return ((a // 2 + b // 2) % 2) * 2 + (a + b) % 2


def choose(values, i):
    if isinstance(i, int):
        return values[i]
    found = values[0]
    for n, value in enumerate(values[1:], 1):
        found = jnp.where(i == n, value, found)
    return found


def plane(i, z):
    other, k = (
        jnp.where(z < HALF, choose([e[n] for e in ORDER[0]], i), choose([e[n] for e in ORDER[1]], i)) for n in range(2)
    )
    return HALF * ((z // HALF + other) % 2) + apart(z % HALF, k)


def score_block(query_block, row_at, passages):
    token = lax.broadcasted_iota(jnp.int32, (8, LANES), 0)
    best = []
    for first in range(0, LANES, GROUP):
        picked = [passages[row_at(first + k) & 255] for k in range(GROUP)]
        sims = lax.dot_general(
            jnp.concatenate(picked, 0), query_block, (((1,), (1,)), ((), ())), preferred_element_type=jnp.float32
        ).reshape(GROUP, PTOK // 8, 8, LANES)
        head = jnp.max(sims[:, : PTOK // 8 - 1], axis=1)
        tail = jnp.where(token[None] < PLEN - (PTOK - 8), sims[:, PTOK // 8 - 1], -jnp.inf)
        best.append(jnp.max(jnp.maximum(head, tail), axis=1))
    best = jnp.concatenate(best, 0)
    slot = lax.broadcasted_iota(jnp.int32, (LANES, LANES), 0)
    lane = lax.broadcasted_iota(jnp.int32, (LANES, LANES), 1)
    own = jnp.where(slot // CAP == lane // QTOK, best, 0.0)
    mean = jnp.sum(own, axis=1, keepdims=True) * (1.0 / QTOK)
    return jnp.sum(jnp.where(slot == lane, mean, 0.0), axis=0, keepdims=True)


def kernel(queries, passages, cand_rows, out, held, held_rows, own_for, corpus, rows_v, rows_s, score_out,
           score_in, own_rows, load_sem, in_sem, rows_sem, q_send, q_recv, r_send, r_recv, s_send, s_recv,
           ready_z, ready_y):
    me = lax.axis_index("shard")
    z, y = me // NY, me % NY

    def send(rows, s, to):
        for src, ref, send_sem, recv_sem in ((rows, held_rows, r_send, r_recv), (held.at[s], held, q_send, q_recv)):
            pltpu.make_async_remote_copy(
                src_ref=src, dst_ref=ref.at[s], send_sem=send_sem, recv_sem=recv_sem.at[s],
                device_id={"shard": to}, device_id_type=MESH).start()

    def send_own(to):
        send(own_for.at[to // NY], me, to)

    def wait_rows(s):
        pltpu.make_async_copy(held_rows.at[s], held_rows.at[s], r_recv.at[s]).wait()

    def wait_block(s):
        pltpu.make_async_copy(held.at[s], held.at[s], q_recv.at[s]).wait()

    def send_score(s):
        @pl.when(s != me)
        def _():
            pltpu.make_async_remote_copy(
                src_ref=score_out.at[s], dst_ref=score_in.at[me], send_sem=s_send, recv_sem=s_recv,
                device_id={"shard": s}, device_id_type=MESH).start()

    def spread(i):
        s = plane(i, z) * NY + y
        wait_rows(s)
        wait_block(s)
        for dy in (2, 1, 3):
            send(held_rows.at[s], s, z * NY + (y + dy) % NY)

    def unpack_rows(i):
        for dy in range(1, NY):
            wait_rows(plane(i, z) * NY + (y + dy) % NY)
        mine = lax.broadcasted_iota(jnp.int32, (16, LANES), 0) == y
        for j in range(NY):
            rows = held_rows[plane(i, z) * NY + j].astype(jnp.float32)
            rows_v[i, j : j + 1] = jnp.sum(jnp.where(mine, rows, 0.0), axis=0, keepdims=True).astype(jnp.int32)
        pltpu.make_async_copy(rows_v.at[i], rows_s.at[i], rows_sem.at[i]).start()

    rows_in = pltpu.make_async_copy(cand_rows, own_rows, in_sem.at[0])
    queries_in = pltpu.make_async_copy(queries, held.at[me], in_sem.at[1])
    rows_in.start()
    queries_in.start()
    loads = []
    part = passages.shape[0] // 4
    for k in range(4):
        span = pl.ds(k * part, part)
        loads.append(pltpu.make_async_copy(passages.at[span], corpus.at[span], load_sem.at[k]))
        loads[-1].start()

    barrier = pltpu.get_barrier_semaphore()
    for d in range(1, NZ):
        to = (z + d) % NZ

        @pl.when(to > z)
        def _():
            pl.semaphore_signal(barrier, inc=1, device_id={"shard": to * NY + y}, device_id_type=MESH)

    for d in range(1, NY):
        to = (y + d) % NY

        @pl.when(to > y)
        def _():
            pl.semaphore_signal(barrier, inc=1, device_id={"shard": z * NY + to}, device_id_type=MESH)

    rows_in.wait()
    packed = jnp.concatenate([own_rows[q] for q in range(4)], axis=1).astype(jnp.float32)
    for to in range(NZ):
        piece = jnp.concatenate([packed[to * NY : (to + 1) * NY], jnp.zeros((16 - NY, LANES), jnp.float32)], axis=0)
        own_for[to] = piece.astype(jnp.bfloat16)
    held_rows[me] = own_for[z]
    queries_in.wait()

    @pl.when(me > 0)
    def _():
        pl.semaphore_wait(barrier, z + y)

    for to in range(NY):

        @pl.when(to < y)
        def _():
            pl.semaphore_signal(ready_y.at[y], inc=1, device_id={"shard": z * NY + to}, device_id_type=MESH)

    for to in range(NZ):

        @pl.when(to < z)
        def _():
            pl.semaphore_signal(ready_z.at[z], inc=1, device_id={"shard": to * NY + y}, device_id_type=MESH)

    for d in (1, 3, 2):
        to = apart(y, d)

        @pl.when(to < y)
        def _():
            send_own(z * NY + to)

    for k in (1, 2, 3):
        to = z - z % HALF + apart(z % HALF, k)

        @pl.when(to < z)
        def _():
            send_own(to * NY + y)

    def send_y(d):
        to = apart(y, d)

        @pl.when(to > y)
        def _():
            pl.semaphore_wait(ready_y.at[to], 1)
            send_own(z * NY + to)

    def send_z(other, k):
        to = HALF * ((z // HALF + other) % 2) + apart(z % HALF, k)

        @pl.when(to > z)
        def _():
            pl.semaphore_wait(ready_z.at[to], 1)
            send_own(to * NY + y)

        if other:

            @pl.when(to < z)
            def _():
                send_own(to * NY + y)

    def send_at(at, now=True):
        for here in range(NZ):
            if at in SENDS[here]:

                @pl.when((z == here) & now)
                def _(here=here):
                    for kind, what in SENDS[here][at]:
                        if kind == "y":
                            send_y(what)
                        elif kind == "o":
                            send_z(*what)
                        else:
                            spread(what)

    send_at(-1)
    unpack_rows(0)
    for load in loads:
        load.wait()

    def step(i, _):
        for at in range(NZ):
            send_at(at, i == at)

        @pl.when(i > 0)
        def _():
            for j in range(NY):
                send_score(plane(i - 1, z) * NY + j)

        rows_at = jnp.where(z < HALF, choose(ROWS_AT[0], i), choose(ROWS_AT[1], i))
        later = jnp.minimum(i + 1, NZ - 1)
        later_at = jnp.where(z < HALF, choose(ROWS_AT[0], later), choose(ROWS_AT[1], later))

        @pl.when(rows_at == i)
        def _():
            unpack_rows(i)

        @pl.when((i + 1 < NZ) & (later_at == i))
        def _():
            unpack_rows(i + 1)

        for dy in range(1, NY):
            wait_block(plane(i, z) * NY + (y + dy) % NY)
        pltpu.make_async_copy(rows_v.at[i], rows_s.at[i], rows_sem.at[i]).wait()
        for j in range(NY):
            s = plane(i, z) * NY + j
            score_out[s] = score_block(held[s], lambda k, j=j: rows_s[i, j, k], corpus)
        return 0

    lax.fori_loop(0, NZ, step, 0)
    for j in range(NY):
        send_score(plane(NZ - 1, z) * NY + j)
    others = pl.ds(0, N - 1)
    pltpu.make_async_copy(score_in.at[others], score_in.at[others], s_recv).wait()
    score_in[me] = score_out[me]
    returned = score_in[...].reshape(N, LANES)
    for q in range(4):
        out[q] = returned[:, q * CAP : (q + 1) * CAP]
    pltpu.make_async_copy(held.at[others], held.at[others], q_send).wait()
    pltpu.make_async_copy(held_rows.at[others], held_rows.at[others], r_send).wait()
    pltpu.make_async_copy(score_in.at[others], score_in.at[others], s_send).wait()


def body(queries, passages, cand_rows, cand_counts):
    count = queries.shape[0]
    block = queries.reshape(count * QTOK, queries.shape[2])
    hbm = pl.BlockSpec(memory_space=pltpu.HBM)
    dma = pltpu.SemaphoreType.DMA
    regular = pltpu.SemaphoreType.REGULAR
    returned = pl.pallas_call(
        kernel,
        out_shape=jax.ShapeDtypeStruct((count, N, CAP), jnp.float32),
        in_specs=[hbm, hbm, hbm],
        out_specs=pl.BlockSpec(memory_space=pltpu.VMEM),
        scratch_shapes=[
            pltpu.VMEM((N,) + block.shape, jnp.bfloat16),
            pltpu.VMEM((N, 16, LANES), jnp.bfloat16),
            pltpu.VMEM((NZ, 16, LANES), jnp.bfloat16),
            pltpu.VMEM(passages.shape, jnp.bfloat16),
            pltpu.VMEM((NZ, NY, LANES), jnp.int32),
            pltpu.SMEM((NZ, NY, LANES), jnp.int32),
            pltpu.VMEM((N, 1, LANES), jnp.float32),
            pltpu.VMEM((N, 1, LANES), jnp.float32),
            pltpu.VMEM(cand_rows.shape, jnp.int32),
            dma((4,)), dma((2,)), dma((NZ,)),
            dma, dma((N,)), dma, dma((N,)), dma, dma,
            regular((NZ,)), regular((NY,)),
        ],
        compiler_params=pltpu.CompilerParams(collective_id=0, has_side_effects=True, vmem_limit_bytes=(64 << 20) - (64 << 10)),
        cost_estimate=pl.CostEstimate(flops=2 * 4096 * 72 * 32 * 128, bytes_accessed=6 << 20, transcendentals=0),
        name="maxsim",
    )(block, passages, cand_rows)
    live = jnp.arange(CAP)[None, None, :] < cand_counts[:, :, None]
    return jnp.where(live, returned, jnp.float32(0.0))


def solution(mesh):
    return jax.shard_map(
        body,
        mesh=mesh,
        in_specs=(
            P(("shard", "rep"), None, None),
            P("shard", None, None),
            P(("shard", "rep"), None, None),
            P(("shard", "rep"), None),
        ),
        out_specs=P(("shard", "rep"), None, None),
        check_vma=False,
    )
```

```python
import jax
import jax.numpy as jnp
from jax import lax
from jax.experimental import pallas as pl
from jax.experimental.pallas import tpu as pltpu
from jax.sharding import PartitionSpec as P

PLEN = 70
PTOK = 72
NZ = 8
NY = 4
HALF = NZ // 2
N = NZ * NY
CAP = 32
QTOK = 32
LANES = 128
GROUP = 16
MESH = pl.DeviceIdType.MESH


ORDER = (
    ((0, 0), (0, 3), (1, 3), (0, 2), (1, 2), (0, 1), (1, 0), (1, 1)),
    ((0, 0), (0, 2), (1, 1), (1, 3), (1, 0), (1, 2), (0, 3), (0, 1)),
)
SENDS = (
    {
        -1: (("y", 3), ("o", (0, 3)), ("y", 1), ("y", 2), ("o", (0, 2)), ("o", (1, 3)),),
        0: (("s", 1), ("o", (1, 1)), ("s", 3), ("o", (0, 1)),),
        1: (("o", (1, 2)), ("s", 2), ("o", (1, 0)),),
        2: (("s", 6), ("s", 4),),
        3: (("s", 5),),
        4: (("s", 7),),
    },
    {
        -1: (("y", 3), ("o", (0, 3)), ("y", 1), ("y", 2), ("o", (0, 2)), ("o", (1, 3)),),
        0: (("s", 1), ("o", (1, 1)), ("s", 3), ("o", (0, 1)),),
        1: (("o", (1, 2)), ("s", 2), ("o", (1, 0)),),
        2: (("s", 6), ("s", 4),),
        3: (("s", 5),),
        4: (("s", 7),),
    },
    {
        -1: (("y", 3), ("o", (0, 3)), ("y", 1), ("y", 2), ("o", (0, 2)), ("o", (1, 3)),),
        0: (("s", 1), ("o", (1, 1)), ("s", 3), ("o", (0, 1)),),
        1: (("o", (1, 2)), ("s", 2), ("o", (1, 0)),),
        2: (("s", 6), ("s", 4),),
        3: (("s", 5),),
        4: (("s", 7),),
    },
    {
        -1: (("y", 3), ("o", (0, 3)), ("y", 1), ("y", 2), ("o", (0, 2)), ("o", (1, 3)),),
        0: (("s", 1), ("o", (1, 1)), ("s", 3), ("o", (0, 1)),),
        1: (("o", (1, 2)), ("s", 2), ("o", (1, 0)),),
        2: (("s", 6), ("s", 4),),
        3: (("s", 5),),
        4: (("s", 7),),
    },
    {
        -1: (("y", 1), ("o", (0, 2)), ("y", 3), ("y", 2), ("o", (1, 3)), ("o", (1, 2)), ("s", 1), ("o", (1, 0)),),
        0: (("s", 3),),
        1: (("o", (0, 3)), ("s", 2), ("o", (0, 1)),),
        2: (("o", (1, 1)), ("s", 4), ("s", 5),),
        3: (("s", 6),),
        4: (("s", 7),),
    },
    {
        -1: (("y", 1), ("o", (0, 2)), ("y", 3), ("y", 2), ("o", (1, 3)), ("o", (1, 2)), ("s", 1), ("o", (1, 0)),),
        0: (("s", 3),),
        1: (("o", (0, 3)), ("s", 2), ("o", (0, 1)),),
        2: (("o", (1, 1)), ("s", 4), ("s", 5),),
        3: (("s", 6),),
        4: (("s", 7),),
    },
    {
        -1: (("y", 1), ("o", (0, 2)), ("y", 3), ("y", 2), ("o", (1, 3)), ("o", (1, 2)), ("s", 1), ("o", (1, 0)),),
        0: (("s", 3),),
        1: (("o", (0, 3)), ("s", 2), ("o", (0, 1)),),
        2: (("o", (1, 1)), ("s", 4), ("s", 5),),
        3: (("s", 6),),
        4: (("s", 7),),
    },
    {
        -1: (("y", 1), ("o", (0, 2)), ("y", 3), ("y", 2), ("o", (1, 3)), ("o", (1, 2)), ("s", 1), ("o", (1, 0)),),
        0: (("s", 3),),
        1: (("o", (0, 3)), ("s", 2), ("o", (0, 1)),),
        2: (("o", (1, 1)), ("s", 4), ("s", 5),),
        3: (("s", 6),),
        4: (("s", 7),),
    },
)
ROWS_AT = (
    (-1, 1, 2, 2, 4, 5, 5, 6),
    (-1, 1, 2, 2, 3, 4, 5, 6),
)


def apart(a, b):
    return ((a // 2 + b // 2) % 2) * 2 + (a + b) % 2


def choose(values, i):
    if isinstance(i, int):
        return values[i]
    found = values[0]
    for n, value in enumerate(values[1:], 1):
        found = jnp.where(i == n, value, found)
    return found


def plane(n, z):
    (low, near), (high, far) = ORDER[0][n], ORDER[1][n]
    other, k = jnp.where(z < HALF, low, high), jnp.where(z < HALF, near, far)
    return HALF * ((z // HALF + other) % 2) + apart(z % HALF, k)


def score_block(query_block, row_at, passages):
    token = lax.broadcasted_iota(jnp.int32, (8, LANES), 0)
    best = []
    for first in range(0, LANES, GROUP):
        picked = [passages[row_at(first + k) & 255] for k in range(GROUP)]
        sims = lax.dot_general(
            jnp.concatenate(picked, 0), query_block, (((1,), (1,)), ((), ())), preferred_element_type=jnp.float32
        ).reshape(GROUP, PTOK // 8, 8, LANES)
        head = jnp.max(sims[:, : PTOK // 8 - 1], axis=1)
        tail = jnp.where(token[None] < PLEN - (PTOK - 8), sims[:, PTOK // 8 - 1], -jnp.inf)
        best.append(jnp.max(jnp.maximum(head, tail), axis=1))
    best = jnp.concatenate(best, 0)
    slot = lax.broadcasted_iota(jnp.int32, (LANES, LANES), 0)
    lane = lax.broadcasted_iota(jnp.int32, (LANES, LANES), 1)
    own = jnp.where(slot // CAP == lane // QTOK, best, 0.0)
    mean = jnp.sum(own, axis=1, keepdims=True) * (1.0 / QTOK)
    return jnp.sum(jnp.where(slot == lane, mean, 0.0), axis=0, keepdims=True)


def kernel(queries, passages, cand_rows, out, held, held_rows, own_for, corpus, rows_v, rows_s, score_out,
           score_in, own_rows, load_sem, in_sem, rows_sem, q_send, q_recv, r_send, r_recv, s_send, s_recv,
           ready_z, ready_y):
    me = lax.axis_index("shard")
    z, y = me // NY, me % NY
    bases = [plane(n, z) * NY for n in range(NZ)]
    others_y = [(y + dy) % NY for dy in range(1, NY)]

    def send(rows, s, to):
        for src, ref, send_sem, recv_sem in ((rows, held_rows, r_send, r_recv), (held.at[s], held, q_send, q_recv)):
            pltpu.make_async_remote_copy(
                src_ref=src, dst_ref=ref.at[s], send_sem=send_sem, recv_sem=recv_sem.at[s],
                device_id={"shard": to}, device_id_type=MESH).start()

    def send_own(to):
        send(own_for.at[to // NY], me, to)

    def wait_rows(s):
        pltpu.make_async_copy(held_rows.at[s], held_rows.at[s], r_recv.at[s]).wait()

    def wait_block(s):
        pltpu.make_async_copy(held.at[s], held.at[s], q_recv.at[s]).wait()

    def send_score(s):
        @pl.when(s != me)
        def _():
            pltpu.make_async_remote_copy(
                src_ref=score_out.at[s], dst_ref=score_in.at[me], send_sem=s_send, recv_sem=s_recv,
                device_id={"shard": s}, device_id_type=MESH).start()

    def spread(i):
        s = bases[i] + y
        wait_rows(s)
        wait_block(s)
        for dy in (2, 1, 3):
            send(held_rows.at[s], s, z * NY + others_y[dy - 1])

    def unpack_rows(i):
        base = choose(bases, i)
        for other in others_y:
            wait_rows(base + other)
        mine = lax.broadcasted_iota(jnp.int32, (16, LANES), 0) == y
        for j in range(NY):
            rows = held_rows[base + j].astype(jnp.float32)
            rows_v[i, j : j + 1] = jnp.sum(jnp.where(mine, rows, 0.0), axis=0, keepdims=True).astype(jnp.int32)
        pltpu.make_async_copy(rows_v.at[i], rows_s.at[i], rows_sem.at[i]).start()

    rows_in = pltpu.make_async_copy(cand_rows, own_rows, in_sem.at[0])
    queries_in = pltpu.make_async_copy(queries, held.at[me], in_sem.at[1])
    rows_in.start()
    queries_in.start()
    loads = []
    part = passages.shape[0] // 4
    for k in range(4):
        span = pl.ds(k * part, part)
        loads.append(pltpu.make_async_copy(passages.at[span], corpus.at[span], load_sem.at[k]))
        loads[-1].start()

    barrier = pltpu.get_barrier_semaphore()
    for d in range(1, NZ):
        to = (z + d) % NZ

        @pl.when(to > z)
        def _():
            pl.semaphore_signal(barrier, inc=1, device_id={"shard": to * NY + y}, device_id_type=MESH)

    for d in range(1, NY):
        to = (y + d) % NY

        @pl.when(to > y)
        def _():
            pl.semaphore_signal(barrier, inc=1, device_id={"shard": z * NY + to}, device_id_type=MESH)

    rows_in.wait()
    packed = jnp.concatenate([own_rows[q] for q in range(4)], axis=1).astype(jnp.float32)
    for to in range(NZ):
        piece = jnp.concatenate([packed[to * NY : (to + 1) * NY], jnp.zeros((16 - NY, LANES), jnp.float32)], axis=0)
        own_for[to] = piece.astype(jnp.bfloat16)
    held_rows[me] = own_for[z]
    queries_in.wait()

    @pl.when(me > 0)
    def _():
        pl.semaphore_wait(barrier, z + y)

    for to in range(NY):

        @pl.when(to < y)
        def _():
            pl.semaphore_signal(ready_y.at[y], inc=1, device_id={"shard": z * NY + to}, device_id_type=MESH)

    for to in range(NZ):

        @pl.when(to < z)
        def _():
            pl.semaphore_signal(ready_z.at[z], inc=1, device_id={"shard": to * NY + y}, device_id_type=MESH)

    for d in (1, 3, 2):
        to = apart(y, d)

        @pl.when(to < y)
        def _():
            send_own(z * NY + to)

    for k in (1, 2, 3):
        to = z - z % HALF + apart(z % HALF, k)

        @pl.when(to < z)
        def _():
            send_own(to * NY + y)

    def send_y(d):
        to = apart(y, d)

        @pl.when(to > y)
        def _():
            pl.semaphore_wait(ready_y.at[to], 1)
            send_own(z * NY + to)

    def send_z(other, k):
        to = HALF * ((z // HALF + other) % 2) + apart(z % HALF, k)

        @pl.when(to > z)
        def _():
            pl.semaphore_wait(ready_z.at[to], 1)
            send_own(to * NY + y)

        if other:

            @pl.when(to < z)
            def _():
                send_own(to * NY + y)

    def send_at(at):
        for here in range(NZ):
            if at in SENDS[here]:

                @pl.when(z == here)
                def _(here=here):
                    for kind, what in SENDS[here][at]:
                        if kind == "y":
                            send_y(what)
                        elif kind == "o":
                            send_z(*what)
                        else:
                            spread(what)

    send_at(-1)
    unpack_rows(0)
    for load in loads:
        load.wait()

    def early(i):
        low, high = (sum((i == k).astype(jnp.int32) for k in range(1, NZ) if at[k] < k) for at in ROWS_AT)
        return jnp.where(z < HALF, low, high) == 1

    def step(i, _):
        @pl.when(i > 0)
        def _():
            base = choose(bases, i - 1)
            for j in range(NY):
                send_score(base + j)

        for at in range(NZ):
            if any(at in SENDS[here] for here in range(NZ)):

                @pl.when(i == at)
                def _(at=at):
                    send_at(at)

        @pl.when((i > 0) & jnp.logical_not(early(i)))
        def _():
            unpack_rows(i)

        @pl.when(early(i + 1))
        def _():
            unpack_rows(i + 1)

        base = choose(bases, i)
        for other in others_y:
            wait_block(base + other)
        pltpu.make_async_copy(rows_v.at[i], rows_s.at[i], rows_sem.at[i]).wait()
        for j in range(NY):
            score_out[base + j] = score_block(held[base + j], lambda k, j=j: rows_s[i, j, k], corpus)
        return 0

    lax.fori_loop(0, NZ, step, 0)
    for j in range(NY):
        send_score(bases[NZ - 1] + j)
    others = pl.ds(0, N - 1)
    pltpu.make_async_copy(score_in.at[others], score_in.at[others], s_recv).wait()
    score_in[me] = score_out[me]
    returned = score_in[...].reshape(N, LANES)
    for q in range(4):
        out[q] = returned[:, q * CAP : (q + 1) * CAP]
    pltpu.make_async_copy(held.at[others], held.at[others], q_send).wait()
    pltpu.make_async_copy(held_rows.at[others], held_rows.at[others], r_send).wait()
    pltpu.make_async_copy(score_in.at[others], score_in.at[others], s_send).wait()


def body(queries, passages, cand_rows, cand_counts):
    count = queries.shape[0]
    block = queries.reshape(count * QTOK, queries.shape[2])
    hbm = pl.BlockSpec(memory_space=pltpu.HBM)
    dma = pltpu.SemaphoreType.DMA
    regular = pltpu.SemaphoreType.REGULAR
    returned = pl.pallas_call(
        kernel,
        out_shape=jax.ShapeDtypeStruct((count, N, CAP), jnp.float32),
        in_specs=[hbm, hbm, hbm],
        out_specs=pl.BlockSpec(memory_space=pltpu.VMEM),
        scratch_shapes=[
            pltpu.VMEM((N,) + block.shape, jnp.bfloat16),
            pltpu.VMEM((N, 16, LANES), jnp.bfloat16),
            pltpu.VMEM((NZ, 16, LANES), jnp.bfloat16),
            pltpu.VMEM(passages.shape, jnp.bfloat16),
            pltpu.VMEM((NZ, NY, LANES), jnp.int32),
            pltpu.SMEM((NZ, NY, LANES), jnp.int32),
            pltpu.VMEM((N, 1, LANES), jnp.float32),
            pltpu.VMEM((N, 1, LANES), jnp.float32),
            pltpu.VMEM(cand_rows.shape, jnp.int32),
            dma((4,)), dma((2,)), dma((NZ,)),
            dma, dma((N,)), dma, dma((N,)), dma, dma,
            regular((NZ,)), regular((NY,)),
        ],
        compiler_params=pltpu.CompilerParams(collective_id=0, has_side_effects=True, vmem_limit_bytes=(64 << 20) - (64 << 10)),
        cost_estimate=pl.CostEstimate(flops=2 * 4096 * 72 * 32 * 128, bytes_accessed=6 << 20, transcendentals=0),
        name="maxsim",
    )(block, passages, cand_rows)
    live = jnp.arange(CAP)[None, None, :] < cand_counts[:, :, None]
    return jnp.where(live, returned, jnp.float32(0.0))


def solution(mesh):
    return jax.shard_map(
        body,
        mesh=mesh,
        in_specs=(
            P(("shard", "rep"), None, None),
            P("shard", None, None),
            P(("shard", "rep"), None, None),
            P(("shard", "rep"), None),
        ),
        out_specs=P(("shard", "rep"), None, None),
        check_vma=False,
    )
```

```python
import jax
import jax.numpy as jnp
from jax import lax
from jax.experimental import pallas as pl
from jax.experimental.pallas import tpu as pltpu
from jax.sharding import PartitionSpec as P

PLEN = 70
PTOK = 72
NZ = 8
NY = 4
HALF = NZ // 2
N = NZ * NY
CAP = 32
QTOK = 32
LANES = 128
GROUP = 16
MESH = pl.DeviceIdType.MESH


ORDER = (
    ((0, 0), (0, 3), (1, 3), (0, 2), (1, 2), (0, 1), (1, 0), (1, 1)),
    ((0, 0), (0, 2), (1, 1), (1, 3), (1, 0), (1, 2), (0, 3), (0, 1)),
)
SENDS = (
    {
        -1: (("y", 3), ("o", (0, 3)), ("y", 1), ("y", 2), ("o", (0, 2)), ("o", (1, 3)),),
        0: (("s", 1), ("o", (1, 1)), ("s", 3), ("o", (0, 1)),),
        1: (("o", (1, 2)), ("s", 2), ("o", (1, 0)),),
        2: (("s", 6), ("s", 4),),
        3: (("s", 5),),
        4: (("s", 7),),
    },
    {
        -1: (("y", 3), ("o", (0, 3)), ("y", 1), ("y", 2), ("o", (0, 2)), ("o", (1, 3)),),
        0: (("s", 1), ("o", (1, 1)), ("s", 3), ("o", (0, 1)),),
        1: (("o", (1, 2)), ("s", 2), ("o", (1, 0)),),
        2: (("s", 6), ("s", 4),),
        3: (("s", 5),),
        4: (("s", 7),),
    },
    {
        -1: (("y", 3), ("o", (0, 3)), ("y", 1), ("y", 2), ("o", (0, 2)), ("o", (1, 3)),),
        0: (("s", 1), ("o", (1, 1)), ("s", 3), ("o", (0, 1)),),
        1: (("o", (1, 2)), ("s", 2), ("o", (1, 0)),),
        2: (("s", 6), ("s", 4),),
        3: (("s", 5),),
        4: (("s", 7),),
    },
    {
        -1: (("y", 3), ("o", (0, 3)), ("y", 1), ("y", 2), ("o", (0, 2)), ("o", (1, 3)),),
        0: (("s", 1), ("o", (1, 1)), ("s", 3), ("o", (0, 1)),),
        1: (("o", (1, 2)), ("s", 2), ("o", (1, 0)),),
        2: (("s", 6), ("s", 4),),
        3: (("s", 5),),
        4: (("s", 7),),
    },
    {
        -1: (("y", 1), ("o", (0, 2)), ("y", 3), ("y", 2), ("o", (1, 3)), ("o", (1, 2)), ("s", 1), ("o", (1, 0)),),
        0: (("s", 3),),
        1: (("o", (0, 3)), ("s", 2), ("o", (0, 1)),),
        2: (("o", (1, 1)), ("s", 4), ("s", 5),),
        3: (("s", 6),),
        4: (("s", 7),),
    },
    {
        -1: (("y", 1), ("o", (0, 2)), ("y", 3), ("y", 2), ("o", (1, 3)), ("o", (1, 2)), ("s", 1), ("o", (1, 0)),),
        0: (("s", 3),),
        1: (("o", (0, 3)), ("s", 2), ("o", (0, 1)),),
        2: (("o", (1, 1)), ("s", 4), ("s", 5),),
        3: (("s", 6),),
        4: (("s", 7),),
    },
    {
        -1: (("y", 1), ("o", (0, 2)), ("y", 3), ("y", 2), ("o", (1, 3)), ("o", (1, 2)), ("s", 1), ("o", (1, 0)),),
        0: (("s", 3),),
        1: (("o", (0, 3)), ("s", 2), ("o", (0, 1)),),
        2: (("o", (1, 1)), ("s", 4), ("s", 5),),
        3: (("s", 6),),
        4: (("s", 7),),
    },
    {
        -1: (("y", 1), ("o", (0, 2)), ("y", 3), ("y", 2), ("o", (1, 3)), ("o", (1, 2)), ("s", 1), ("o", (1, 0)),),
        0: (("s", 3),),
        1: (("o", (0, 3)), ("s", 2), ("o", (0, 1)),),
        2: (("o", (1, 1)), ("s", 4), ("s", 5),),
        3: (("s", 6),),
        4: (("s", 7),),
    },
)
ROWS_AT = (
    (-1, 1, 2, 2, 4, 5, 5, 6),
    (-1, 1, 2, 2, 3, 4, 5, 6),
)


def apart(a, b):
    return ((a // 2 + b // 2) % 2) * 2 + (a + b) % 2


def choose(values, i):
    if isinstance(i, int):
        return values[i]
    found = values[0]
    for n, value in enumerate(values[1:], 1):
        found = jnp.where(i == n, value, found)
    return found


def plane(n, z):
    (low, near), (high, far) = ORDER[0][n], ORDER[1][n]
    other, k = jnp.where(z < HALF, low, high), jnp.where(z < HALF, near, far)
    return HALF * ((z // HALF + other) % 2) + apart(z % HALF, k)


def score_block(query_block, row_at, passages):
    token = lax.broadcasted_iota(jnp.int32, (8, LANES), 0)
    best = []
    for first in range(0, LANES, GROUP):
        picked = [passages[row_at(first + k) & 255] for k in range(GROUP)]
        sims = lax.dot_general(
            jnp.concatenate(picked, 0), query_block, (((1,), (1,)), ((), ())), preferred_element_type=jnp.float32
        ).reshape(GROUP, PTOK // 8, 8, LANES)
        head = jnp.max(sims[:, : PTOK // 8 - 1], axis=1)
        tail = jnp.where(token[None] < PLEN - (PTOK - 8), sims[:, PTOK // 8 - 1], -jnp.inf)
        best.append(jnp.max(jnp.maximum(head, tail), axis=1))
    best = jnp.concatenate(best, 0)
    slot = lax.broadcasted_iota(jnp.int32, (LANES, LANES), 0)
    lane = lax.broadcasted_iota(jnp.int32, (LANES, LANES), 1)
    own = jnp.where(slot // CAP == lane // QTOK, best, 0.0)
    mean = jnp.sum(own, axis=1, keepdims=True) * (1.0 / QTOK)
    return jnp.sum(jnp.where(slot == lane, mean, 0.0), axis=0, keepdims=True)


def kernel(queries, passages, cand_rows, out, held, held_rows, own_for, corpus, rows_v, rows_s, score_out,
           score_in, own_rows, load_sem, in_sem, rows_sem, q_send, q_recv, r_send, r_recv, s_send, s_recv,
           ready_z, ready_y):
    me = lax.axis_index("shard")
    z, y = me // NY, me % NY
    bases = [plane(n, z) * NY for n in range(NZ)]
    others_y = [(y + dy) % NY for dy in range(1, NY)]

    def send(rows, s, to):
        for src, ref, send_sem, recv_sem in ((rows, held_rows, r_send, r_recv), (held.at[s], held, q_send, q_recv)):
            pltpu.make_async_remote_copy(
                src_ref=src, dst_ref=ref.at[s], send_sem=send_sem, recv_sem=recv_sem.at[s],
                device_id={"shard": to}, device_id_type=MESH).start()

    def send_own(to):
        send(own_for.at[to // NY], me, to)

    def wait_rows(s):
        pltpu.make_async_copy(held_rows.at[s], held_rows.at[s], r_recv.at[s]).wait()

    def wait_block(s):
        pltpu.make_async_copy(held.at[s], held.at[s], q_recv.at[s]).wait()

    def send_score(s):
        @pl.when(s != me)
        def _():
            pltpu.make_async_remote_copy(
                src_ref=score_out.at[s], dst_ref=score_in.at[me], send_sem=s_send, recv_sem=s_recv,
                device_id={"shard": s}, device_id_type=MESH).start()

    def spread(i):
        s = bases[i] + y
        wait_rows(s)
        wait_block(s)
        for dy in (2, 1, 3):
            send(held_rows.at[s], s, z * NY + others_y[dy - 1])

    def unpack_rows(i):
        base = choose(bases, i)
        for other in others_y:
            wait_rows(base + other)
        mine = lax.broadcasted_iota(jnp.int32, (16, LANES), 0) == y
        for j in range(NY):
            rows = held_rows[base + j].astype(jnp.float32)
            rows_v[i, j : j + 1] = jnp.sum(jnp.where(mine, rows, 0.0), axis=0, keepdims=True).astype(jnp.int32)
        pltpu.make_async_copy(rows_v.at[i], rows_s.at[i], rows_sem.at[i]).start()

    rows_in = pltpu.make_async_copy(cand_rows, own_rows, in_sem.at[0])
    queries_in = pltpu.make_async_copy(queries, held.at[me], in_sem.at[1])
    rows_in.start()
    queries_in.start()
    barrier = pltpu.get_barrier_semaphore()
    for d in range(1, NZ):
        to = (z + d) % NZ

        @pl.when(to > z)
        def _():
            pl.semaphore_signal(barrier, inc=1, device_id={"shard": to * NY + y}, device_id_type=MESH)

    for d in range(1, NY):
        to = (y + d) % NY

        @pl.when(to > y)
        def _():
            pl.semaphore_signal(barrier, inc=1, device_id={"shard": z * NY + to}, device_id_type=MESH)

    loads = []
    part = passages.shape[0] // 4
    for k in range(4):
        span = pl.ds(k * part, part)
        loads.append(pltpu.make_async_copy(passages.at[span], corpus.at[span], load_sem.at[k]))
        loads[-1].start()

    @pl.when(me > 0)
    def _():
        pl.semaphore_wait(barrier, z + y)

    for to in range(NY):

        @pl.when(to < y)
        def _():
            pl.semaphore_signal(ready_y.at[y], inc=1, device_id={"shard": z * NY + to}, device_id_type=MESH)

    for to in range(NZ):

        @pl.when(to < z)
        def _():
            pl.semaphore_signal(ready_z.at[z], inc=1, device_id={"shard": to * NY + y}, device_id_type=MESH)

    rows_in.wait()
    packed = jnp.concatenate([own_rows[q] for q in range(4)], axis=1).astype(jnp.float32)
    for to in range(NZ):
        piece = jnp.concatenate([packed[to * NY : (to + 1) * NY], jnp.zeros((16 - NY, LANES), jnp.float32)], axis=0)
        own_for[to] = piece.astype(jnp.bfloat16)
    held_rows[me] = own_for[z]
    queries_in.wait()

    for d in (1, 3, 2):
        to = apart(y, d)

        @pl.when(to < y)
        def _():
            send_own(z * NY + to)

    for k in (1, 2, 3):
        to = z - z % HALF + apart(z % HALF, k)

        @pl.when(to < z)
        def _():
            send_own(to * NY + y)

    def send_y(d):
        to = apart(y, d)

        @pl.when(to > y)
        def _():
            pl.semaphore_wait(ready_y.at[to], 1)
            send_own(z * NY + to)

    def send_z(other, k):
        to = HALF * ((z // HALF + other) % 2) + apart(z % HALF, k)

        @pl.when(to > z)
        def _():
            pl.semaphore_wait(ready_z.at[to], 1)
            send_own(to * NY + y)

        if other:

            @pl.when(to < z)
            def _():
                send_own(to * NY + y)

    def send_at(at):
        for here in range(NZ):
            if at in SENDS[here]:

                @pl.when(z == here)
                def _(here=here):
                    for kind, what in SENDS[here][at]:
                        if kind == "y":
                            send_y(what)
                        elif kind == "o":
                            send_z(*what)
                        else:
                            spread(what)

    send_at(-1)
    unpack_rows(0)
    for load in loads:
        load.wait()

    def early(i):
        low, high = (sum((i == k).astype(jnp.int32) for k in range(1, NZ) if at[k] < k) for at in ROWS_AT)
        return jnp.where(z < HALF, low, high) == 1

    def step(i, _):
        @pl.when(i > 0)
        def _():
            base = choose(bases, i - 1)
            for j in range(NY):
                send_score(base + j)

        for at in range(NZ):
            if any(at in SENDS[here] for here in range(NZ)):

                @pl.when(i == at)
                def _(at=at):
                    send_at(at)

        @pl.when((i > 0) & jnp.logical_not(early(i)))
        def _():
            unpack_rows(i)

        @pl.when(early(i + 1))
        def _():
            unpack_rows(i + 1)

        base = choose(bases, i)
        for other in others_y:
            wait_block(base + other)
        pltpu.make_async_copy(rows_v.at[i], rows_s.at[i], rows_sem.at[i]).wait()
        for j in range(NY):
            score_out[base + j] = score_block(held[base + j], lambda k, j=j: rows_s[i, j, k], corpus)
        return 0

    lax.fori_loop(0, NZ, step, 0)
    for j in range(NY):
        send_score(bases[NZ - 1] + j)
    others = pl.ds(0, N - 1)
    pltpu.make_async_copy(score_in.at[others], score_in.at[others], s_recv).wait()
    score_in[me] = score_out[me]
    returned = score_in[...].reshape(N, LANES)
    for q in range(4):
        out[q] = returned[:, q * CAP : (q + 1) * CAP]
    pltpu.make_async_copy(held.at[others], held.at[others], q_send).wait()
    pltpu.make_async_copy(held_rows.at[others], held_rows.at[others], r_send).wait()
    pltpu.make_async_copy(score_in.at[others], score_in.at[others], s_send).wait()


def body(queries, passages, cand_rows, cand_counts):
    count = queries.shape[0]
    block = queries.reshape(count * QTOK, queries.shape[2])
    hbm = pl.BlockSpec(memory_space=pltpu.HBM)
    dma = pltpu.SemaphoreType.DMA
    regular = pltpu.SemaphoreType.REGULAR
    returned = pl.pallas_call(
        kernel,
        out_shape=jax.ShapeDtypeStruct((count, N, CAP), jnp.float32),
        in_specs=[hbm, hbm, hbm],
        out_specs=pl.BlockSpec(memory_space=pltpu.VMEM),
        scratch_shapes=[
            pltpu.VMEM((N,) + block.shape, jnp.bfloat16),
            pltpu.VMEM((N, 16, LANES), jnp.bfloat16),
            pltpu.VMEM((NZ, 16, LANES), jnp.bfloat16),
            pltpu.VMEM(passages.shape, jnp.bfloat16),
            pltpu.VMEM((NZ, NY, LANES), jnp.int32),
            pltpu.SMEM((NZ, NY, LANES), jnp.int32),
            pltpu.VMEM((N, 1, LANES), jnp.float32),
            pltpu.VMEM((N, 1, LANES), jnp.float32),
            pltpu.VMEM(cand_rows.shape, jnp.int32),
            dma((4,)), dma((2,)), dma((NZ,)),
            dma, dma((N,)), dma, dma((N,)), dma, dma,
            regular((NZ,)), regular((NY,)),
        ],
        compiler_params=pltpu.CompilerParams(collective_id=0, has_side_effects=True, vmem_limit_bytes=(64 << 20) - (64 << 10)),
        cost_estimate=pl.CostEstimate(flops=2 * 4096 * 72 * 32 * 128, bytes_accessed=6 << 20, transcendentals=0),
        name="maxsim",
    )(block, passages, cand_rows)
    live = jnp.arange(CAP)[None, None, :] < cand_counts[:, :, None]
    return jnp.where(live, returned, jnp.float32(0.0))


def solution(mesh):
    return jax.shard_map(
        body,
        mesh=mesh,
        in_specs=(
            P(("shard", "rep"), None, None),
            P("shard", None, None),
            P(("shard", "rep"), None, None),
            P(("shard", "rep"), None),
        ),
        out_specs=P(("shard", "rep"), None, None),
        check_vma=False,
    )
```

```python
import jax
import jax.numpy as jnp
from jax import lax
from jax.experimental import pallas as pl
from jax.experimental.pallas import tpu as pltpu
from jax.sharding import PartitionSpec as P

PLEN = 70
PTOK = 72
NZ = 8
NY = 4
HALF = NZ // 2
N = NZ * NY
CAP = 32
QTOK = 32
LANES = 128
GROUP = 16
MESH = pl.DeviceIdType.MESH


ORDER = (
    ((0, 0), (0, 3), (1, 3), (0, 2), (1, 2), (0, 1), (1, 0), (1, 1)),
    ((0, 0), (0, 2), (1, 1), (1, 3), (1, 0), (1, 2), (0, 3), (0, 1)),
)
SENDS = (
    {
        -1: (("y", 3), ("o", (0, 3)), ("y", 1), ("y", 2), ("o", (0, 2)), ("o", (1, 3)), ("s", 1),),
        0: (("o", (1, 1)), ("s", 3), ("o", (0, 1)),),
        1: (("o", (1, 2)), ("s", 2), ("o", (1, 0)),),
        2: (("s", 6), ("s", 4),),
        3: (("s", 5),),
        4: (("s", 7),),
    },
    {
        -1: (("y", 3), ("o", (0, 3)), ("y", 1), ("y", 2), ("o", (0, 2)), ("o", (1, 3)), ("s", 1),),
        0: (("o", (1, 1)), ("s", 3), ("o", (0, 1)),),
        1: (("o", (1, 2)), ("s", 2), ("o", (1, 0)),),
        2: (("s", 6), ("s", 4),),
        3: (("s", 5),),
        4: (("s", 7),),
    },
    {
        -1: (("y", 3), ("o", (0, 3)), ("y", 1), ("y", 2), ("o", (0, 2)), ("o", (1, 3)), ("s", 1),),
        0: (("o", (1, 1)), ("s", 3), ("o", (0, 1)),),
        1: (("o", (1, 2)), ("s", 2), ("o", (1, 0)),),
        2: (("s", 6), ("s", 4),),
        3: (("s", 5),),
        4: (("s", 7),),
    },
    {
        -1: (("y", 3), ("o", (0, 3)), ("y", 1), ("y", 2), ("o", (0, 2)), ("o", (1, 3)), ("s", 1),),
        0: (("o", (1, 1)), ("s", 3), ("o", (0, 1)),),
        1: (("o", (1, 2)), ("s", 2), ("o", (1, 0)),),
        2: (("s", 6), ("s", 4),),
        3: (("s", 5),),
        4: (("s", 7),),
    },
    {
        -1: (("y", 1), ("o", (0, 2)), ("y", 3), ("y", 2), ("o", (1, 3)), ("o", (1, 2)), ("s", 1), ("o", (1, 0)),),
        0: (("s", 3),),
        1: (("o", (0, 3)), ("s", 2), ("o", (0, 1)),),
        2: (("o", (1, 1)), ("s", 4), ("s", 5),),
        3: (("s", 6),),
        4: (("s", 7),),
    },
    {
        -1: (("y", 1), ("o", (0, 2)), ("y", 3), ("y", 2), ("o", (1, 3)), ("o", (1, 2)), ("s", 1), ("o", (1, 0)),),
        0: (("s", 3),),
        1: (("o", (0, 3)), ("s", 2), ("o", (0, 1)),),
        2: (("o", (1, 1)), ("s", 4), ("s", 5),),
        3: (("s", 6),),
        4: (("s", 7),),
    },
    {
        -1: (("y", 1), ("o", (0, 2)), ("y", 3), ("y", 2), ("o", (1, 3)), ("o", (1, 2)), ("s", 1), ("o", (1, 0)),),
        0: (("s", 3),),
        1: (("o", (0, 3)), ("s", 2), ("o", (0, 1)),),
        2: (("o", (1, 1)), ("s", 4), ("s", 5),),
        3: (("s", 6),),
        4: (("s", 7),),
    },
    {
        -1: (("y", 1), ("o", (0, 2)), ("y", 3), ("y", 2), ("o", (1, 3)), ("o", (1, 2)), ("s", 1), ("o", (1, 0)),),
        0: (("s", 3),),
        1: (("o", (0, 3)), ("s", 2), ("o", (0, 1)),),
        2: (("o", (1, 1)), ("s", 4), ("s", 5),),
        3: (("s", 6),),
        4: (("s", 7),),
    },
)
ROWS_AT = (
    (-1, 1, 2, 2, 4, 5, 5, 6),
    (-1, 1, 2, 2, 3, 4, 5, 6),
)


def apart(a, b):
    return ((a // 2 + b // 2) % 2) * 2 + (a + b) % 2


def choose(values, i):
    if isinstance(i, int):
        return values[i]
    found = values[0]
    for n, value in enumerate(values[1:], 1):
        found = jnp.where(i == n, value, found)
    return found


def plane(n, z):
    (low, near), (high, far) = ORDER[0][n], ORDER[1][n]
    other, k = jnp.where(z < HALF, low, high), jnp.where(z < HALF, near, far)
    return HALF * ((z // HALF + other) % 2) + apart(z % HALF, k)


def score_block(query_block, row_at, passages):
    token = lax.broadcasted_iota(jnp.int32, (8, LANES), 0)
    best = []
    for first in range(0, LANES, GROUP):
        picked = [passages[row_at(first + k) & 255] for k in range(GROUP)]
        sims = lax.dot_general(
            jnp.concatenate(picked, 0), query_block, (((1,), (1,)), ((), ())), preferred_element_type=jnp.float32
        ).reshape(GROUP, PTOK // 8, 8, LANES)
        head = jnp.max(sims[:, : PTOK // 8 - 1], axis=1)
        tail = jnp.where(token[None] < PLEN - (PTOK - 8), sims[:, PTOK // 8 - 1], -jnp.inf)
        best.append(jnp.max(jnp.maximum(head, tail), axis=1))
    best = jnp.concatenate(best, 0)
    slot = lax.broadcasted_iota(jnp.int32, (LANES, LANES), 0)
    lane = lax.broadcasted_iota(jnp.int32, (LANES, LANES), 1)
    own = jnp.where(slot // CAP == lane // QTOK, best, 0.0)
    mean = jnp.sum(own, axis=1, keepdims=True) * (1.0 / QTOK)
    return jnp.sum(jnp.where(slot == lane, mean, 0.0), axis=0, keepdims=True)


def kernel(queries, passages, cand_rows, out, held, held_rows, own_for, corpus, rows_v, rows_s, score_out,
           score_in, own_rows, load_sem, in_sem, rows_sem, q_send, q_recv, r_send, r_recv, s_send, s_recv,
           ready_z, ready_y):
    me = lax.axis_index("shard")
    z, y = me // NY, me % NY
    bases = [plane(n, z) * NY for n in range(NZ)]
    others_y = [(y + dy) % NY for dy in range(1, NY)]

    def send(rows, s, to):
        for src, ref, send_sem, recv_sem in ((rows, held_rows, r_send, r_recv), (held.at[s], held, q_send, q_recv)):
            pltpu.make_async_remote_copy(
                src_ref=src, dst_ref=ref.at[s], send_sem=send_sem, recv_sem=recv_sem.at[s],
                device_id={"shard": to}, device_id_type=MESH).start()

    def send_own(to):
        send(own_for.at[to // NY], me, to)

    def wait_rows(s):
        pltpu.make_async_copy(held_rows.at[s], held_rows.at[s], r_recv.at[s]).wait()

    def wait_block(s):
        pltpu.make_async_copy(held.at[s], held.at[s], q_recv.at[s]).wait()

    def send_score(s):
        @pl.when(s != me)
        def _():
            pltpu.make_async_remote_copy(
                src_ref=score_out.at[s], dst_ref=score_in.at[me], send_sem=s_send, recv_sem=s_recv,
                device_id={"shard": s}, device_id_type=MESH).start()

    def spread(i):
        s = bases[i] + y
        wait_rows(s)
        wait_block(s)
        for dy in (2, 1, 3):
            send(held_rows.at[s], s, z * NY + others_y[dy - 1])

    def member(i, j):
        return jnp.where(y == j, choose(bases[1:] + bases[-1:], i), choose(bases, i)) + j

    def unpack_rows(i):
        base = bases[i] if isinstance(i, int) else choose(bases, i)
        for other in others_y:
            wait_rows(base + other)
        mine = lax.broadcasted_iota(jnp.int32, (16, LANES), 0) == y
        for j in range(NY):
            rows = held_rows[member(i, j)].astype(jnp.float32)
            rows_v[i, j : j + 1] = jnp.sum(jnp.where(mine, rows, 0.0), axis=0, keepdims=True).astype(jnp.int32)
        pltpu.make_async_copy(rows_v.at[i], rows_s.at[i], rows_sem.at[i]).start()

    rows_in = pltpu.make_async_copy(cand_rows, own_rows, in_sem.at[0])
    queries_in = pltpu.make_async_copy(queries, held.at[me], in_sem.at[1])
    rows_in.start()
    queries_in.start()
    barrier = pltpu.get_barrier_semaphore()
    for d in range(1, NZ):
        to = (z + d) % NZ

        @pl.when(to > z)
        def _():
            pl.semaphore_signal(barrier, inc=1, device_id={"shard": to * NY + y}, device_id_type=MESH)

    for d in range(1, NY):
        to = (y + d) % NY

        @pl.when(to > y)
        def _():
            pl.semaphore_signal(barrier, inc=1, device_id={"shard": z * NY + to}, device_id_type=MESH)

    loads = []
    part = passages.shape[0] // 4
    for k in range(4):
        span = pl.ds(k * part, part)
        loads.append(pltpu.make_async_copy(passages.at[span], corpus.at[span], load_sem.at[k]))
        loads[-1].start()

    @pl.when(me > 0)
    def _():
        pl.semaphore_wait(barrier, z + y)

    for to in range(NY):

        @pl.when(to < y)
        def _():
            pl.semaphore_signal(ready_y.at[y], inc=1, device_id={"shard": z * NY + to}, device_id_type=MESH)

    for to in range(NZ):

        @pl.when(to < z)
        def _():
            pl.semaphore_signal(ready_z.at[z], inc=1, device_id={"shard": to * NY + y}, device_id_type=MESH)

    rows_in.wait()
    packed = jnp.concatenate([own_rows[q] for q in range(4)], axis=1).astype(jnp.float32)
    for to in range(NZ):
        piece = jnp.concatenate([packed[to * NY : (to + 1) * NY], jnp.zeros((16 - NY, LANES), jnp.float32)], axis=0)
        own_for[to] = piece.astype(jnp.bfloat16)
    held_rows[me] = own_for[z]
    queries_in.wait()

    for d in (1, 3, 2):
        to = apart(y, d)

        @pl.when(to < y)
        def _():
            send_own(z * NY + to)

    for k in (1, 2, 3):
        to = z - z % HALF + apart(z % HALF, k)

        @pl.when(to < z)
        def _():
            send_own(to * NY + y)

    def send_y(d):
        to = apart(y, d)

        @pl.when(to > y)
        def _():
            pl.semaphore_wait(ready_y.at[to], 1)
            send_own(z * NY + to)

    def send_z(other, k):
        to = HALF * ((z // HALF + other) % 2) + apart(z % HALF, k)

        @pl.when(to > z)
        def _():
            pl.semaphore_wait(ready_z.at[to], 1)
            send_own(to * NY + y)

        if other:

            @pl.when(to < z)
            def _():
                send_own(to * NY + y)

    def send_at(at):
        for here in range(NZ):
            if at in SENDS[here]:

                @pl.when(z == here)
                def _(here=here):
                    for kind, what in SENDS[here][at]:
                        if kind == "y":
                            send_y(what)
                        elif kind == "o":
                            send_z(*what)
                        else:
                            spread(what)

    mine = lax.broadcasted_iota(jnp.int32, (16, LANES), 0) == y
    own_row = jnp.sum(jnp.where(mine, held_rows[me].astype(jnp.float32), 0.0), axis=0, keepdims=True)
    rows_v[NZ] = jnp.broadcast_to(own_row.astype(jnp.int32), (NY, LANES))
    own_in = pltpu.make_async_copy(rows_v.at[NZ], rows_s.at[NZ], rows_sem.at[NZ])
    own_in.start()
    for load in loads:
        load.wait()
    own_in.wait()
    score_out[me] = score_block(held[me], lambda k: rows_s[NZ, 0, k], corpus)
    send_at(-1)
    unpack_rows(0)

    def early(i):
        low, high = (sum((i == k).astype(jnp.int32) for k in range(1, NZ) if at[k] < k) for at in ROWS_AT)
        return jnp.where(z < HALF, low, high) == 1

    def step(i, _):
        @pl.when(i > 0)
        def _():
            for j in range(NY):
                send_score(member(i - 1, j))

        for at in range(NZ):
            if any(at in SENDS[here] for here in range(NZ)):

                @pl.when(i == at)
                def _(at=at):
                    send_at(at)

        @pl.when((i > 0) & jnp.logical_not(early(i)))
        def _():
            unpack_rows(i)

        @pl.when(early(i + 1))
        def _():
            unpack_rows(i + 1)

        await_others(choose(bases, i))
        pltpu.make_async_copy(rows_v.at[i], rows_s.at[i], rows_sem.at[i]).wait()
        for j in range(NY):
            score_out[member(i, j)] = score_block(held[member(i, j)], lambda k, j=j: rows_s[i, j, k], corpus)
        return 0

    def await_others(base):
        for other in others_y:
            wait_block(base + other)

    last = NZ - 1
    lax.fori_loop(0, last, step, 0)
    for j in range(NY):
        send_score(member(last - 1, j))
    await_others(bases[last])
    pltpu.make_async_copy(rows_v.at[last], rows_s.at[last], rows_sem.at[last]).wait()
    for other in others_y:
        s = bases[last] + other
        score_out[s] = score_block(held[s], lambda k, other=other: rows_s[last, other, k], corpus)
    for other in others_y:
        send_score(bases[last] + other)
    others = pl.ds(0, N - 1)
    pltpu.make_async_copy(score_in.at[others], score_in.at[others], s_recv).wait()
    score_in[me] = score_out[me]
    returned = score_in[...].reshape(N, LANES)
    for q in range(4):
        out[q] = returned[:, q * CAP : (q + 1) * CAP]
    pltpu.make_async_copy(held.at[others], held.at[others], q_send).wait()
    pltpu.make_async_copy(held_rows.at[others], held_rows.at[others], r_send).wait()
    pltpu.make_async_copy(score_in.at[others], score_in.at[others], s_send).wait()


def body(queries, passages, cand_rows, cand_counts):
    count = queries.shape[0]
    block = queries.reshape(count * QTOK, queries.shape[2])
    hbm = pl.BlockSpec(memory_space=pltpu.HBM)
    dma = pltpu.SemaphoreType.DMA
    regular = pltpu.SemaphoreType.REGULAR
    returned = pl.pallas_call(
        kernel,
        out_shape=jax.ShapeDtypeStruct((count, N, CAP), jnp.float32),
        in_specs=[hbm, hbm, hbm],
        out_specs=pl.BlockSpec(memory_space=pltpu.VMEM),
        scratch_shapes=[
            pltpu.VMEM((N,) + block.shape, jnp.bfloat16),
            pltpu.VMEM((N, 16, LANES), jnp.bfloat16),
            pltpu.VMEM((NZ, 16, LANES), jnp.bfloat16),
            pltpu.VMEM(passages.shape, jnp.bfloat16),
            pltpu.VMEM((NZ + 1, NY, LANES), jnp.int32),
            pltpu.SMEM((NZ + 1, NY, LANES), jnp.int32),
            pltpu.VMEM((N, 1, LANES), jnp.float32),
            pltpu.VMEM((N, 1, LANES), jnp.float32),
            pltpu.VMEM(cand_rows.shape, jnp.int32),
            dma((4,)), dma((2,)), dma((NZ + 1,)),
            dma, dma((N,)), dma, dma((N,)), dma, dma,
            regular((NZ,)), regular((NY,)),
        ],
        compiler_params=pltpu.CompilerParams(collective_id=0, has_side_effects=True, vmem_limit_bytes=(64 << 20) - (64 << 10)),
        cost_estimate=pl.CostEstimate(flops=2 * 4096 * 72 * 32 * 128, bytes_accessed=6 << 20, transcendentals=0),
        name="maxsim",
    )(block, passages, cand_rows)
    live = jnp.arange(CAP)[None, None, :] < cand_counts[:, :, None]
    return jnp.where(live, returned, jnp.float32(0.0))


def solution(mesh):
    return jax.shard_map(
        body,
        mesh=mesh,
        in_specs=(
            P(("shard", "rep"), None, None),
            P("shard", None, None),
            P(("shard", "rep"), None, None),
            P(("shard", "rep"), None),
        ),
        out_specs=P(("shard", "rep"), None, None),
        check_vma=False,
    )
```

```python
import jax
import jax.numpy as jnp
from jax import lax
from jax.experimental import pallas as pl
from jax.experimental.pallas import tpu as pltpu
from jax.sharding import PartitionSpec as P

PLEN = 70
PTOK = 72
NZ = 8
NY = 4
HALF = NZ // 2
N = NZ * NY
CAP = 32
QTOK = 32
LANES = 128
GROUP = 16
MESH = pl.DeviceIdType.MESH


ORDER = (
    ((0, 0), (0, 3), (1, 3), (0, 2), (1, 2), (0, 1), (1, 0), (1, 1)),
    ((0, 0), (0, 2), (1, 1), (1, 3), (1, 0), (1, 2), (0, 3), (0, 1)),
)
SENDS = (
    {
        -1: (("y", 3), ("o", (0, 3)), ("y", 1), ("y", 2), ("o", (0, 2)), ("o", (1, 3)), ("s", 1),),
        0: (("o", (1, 1)), ("s", 3), ("o", (0, 1)),),
        1: (("o", (1, 2)), ("s", 2), ("o", (1, 0)),),
        2: (("s", 6), ("s", 4),),
        3: (("s", 5),),
        4: (("s", 7),),
    },
    {
        -1: (("y", 3), ("o", (0, 3)), ("y", 1), ("y", 2), ("o", (0, 2)), ("o", (1, 3)), ("s", 1),),
        0: (("o", (1, 1)), ("s", 3), ("o", (0, 1)),),
        1: (("o", (1, 2)), ("s", 2), ("o", (1, 0)),),
        2: (("s", 6), ("s", 4),),
        3: (("s", 5),),
        4: (("s", 7),),
    },
    {
        -1: (("y", 3), ("o", (0, 3)), ("y", 1), ("y", 2), ("o", (0, 2)), ("o", (1, 3)), ("s", 1),),
        0: (("o", (1, 1)), ("s", 3), ("o", (0, 1)),),
        1: (("o", (1, 2)), ("s", 2), ("o", (1, 0)),),
        2: (("s", 6), ("s", 4),),
        3: (("s", 5),),
        4: (("s", 7),),
    },
    {
        -1: (("y", 3), ("o", (0, 3)), ("y", 1), ("y", 2), ("o", (0, 2)), ("o", (1, 3)), ("s", 1),),
        0: (("o", (1, 1)), ("s", 3), ("o", (0, 1)),),
        1: (("o", (1, 2)), ("s", 2), ("o", (1, 0)),),
        2: (("s", 6), ("s", 4),),
        3: (("s", 5),),
        4: (("s", 7),),
    },
    {
        -1: (("y", 1), ("o", (0, 2)), ("y", 3), ("y", 2), ("o", (1, 3)), ("o", (1, 2)), ("s", 1), ("o", (1, 0)),),
        0: (("s", 3),),
        1: (("o", (0, 3)), ("s", 2), ("o", (0, 1)),),
        2: (("o", (1, 1)), ("s", 4), ("s", 5),),
        3: (("s", 6),),
        4: (("s", 7),),
    },
    {
        -1: (("y", 1), ("o", (0, 2)), ("y", 3), ("y", 2), ("o", (1, 3)), ("o", (1, 2)), ("s", 1), ("o", (1, 0)),),
        0: (("s", 3),),
        1: (("o", (0, 3)), ("s", 2), ("o", (0, 1)),),
        2: (("o", (1, 1)), ("s", 4), ("s", 5),),
        3: (("s", 6),),
        4: (("s", 7),),
    },
    {
        -1: (("y", 1), ("o", (0, 2)), ("y", 3), ("y", 2), ("o", (1, 3)), ("o", (1, 2)), ("s", 1), ("o", (1, 0)),),
        0: (("s", 3),),
        1: (("o", (0, 3)), ("s", 2), ("o", (0, 1)),),
        2: (("o", (1, 1)), ("s", 4), ("s", 5),),
        3: (("s", 6),),
        4: (("s", 7),),
    },
    {
        -1: (("y", 1), ("o", (0, 2)), ("y", 3), ("y", 2), ("o", (1, 3)), ("o", (1, 2)), ("s", 1), ("o", (1, 0)),),
        0: (("s", 3),),
        1: (("o", (0, 3)), ("s", 2), ("o", (0, 1)),),
        2: (("o", (1, 1)), ("s", 4), ("s", 5),),
        3: (("s", 6),),
        4: (("s", 7),),
    },
)
ROWS_AT = (
    (-1, 1, 2, 2, 4, 5, 5, 6),
    (-1, 1, 2, 2, 3, 4, 5, 6),
)


def apart(a, b):
    return ((a // 2 + b // 2) % 2) * 2 + (a + b) % 2


def choose(values, i):
    if isinstance(i, int):
        return values[i]
    found = values[0]
    for n, value in enumerate(values[1:], 1):
        found = jnp.where(i == n, value, found)
    return found


def plane(n, z):
    (low, near), (high, far) = ORDER[0][n], ORDER[1][n]
    other, k = jnp.where(z < HALF, low, high), jnp.where(z < HALF, near, far)
    return HALF * ((z // HALF + other) % 2) + apart(z % HALF, k)


def score_block(query_block, row_at, passages):
    token = lax.broadcasted_iota(jnp.int32, (8, LANES), 0)
    best = []
    for first in range(0, LANES, GROUP):
        picked = [passages[row_at(first + k) & 255] for k in range(GROUP)]
        sims = lax.dot_general(
            jnp.concatenate(picked, 0), query_block, (((1,), (1,)), ((), ())), preferred_element_type=jnp.float32
        ).reshape(GROUP, PTOK // 8, 8, LANES)
        head = jnp.max(sims[:, : PTOK // 8 - 1], axis=1)
        tail = jnp.where(token[None] < PLEN - (PTOK - 8), sims[:, PTOK // 8 - 1], -jnp.inf)
        best.append(jnp.max(jnp.maximum(head, tail), axis=1))
    best = jnp.concatenate(best, 0)
    slot = lax.broadcasted_iota(jnp.int32, (LANES, LANES), 0)
    lane = lax.broadcasted_iota(jnp.int32, (LANES, LANES), 1)
    own = jnp.where(slot // CAP == lane // QTOK, best, 0.0)
    mean = jnp.sum(own, axis=1, keepdims=True) * (1.0 / QTOK)
    return jnp.sum(jnp.where(slot == lane, mean, 0.0), axis=0, keepdims=True)


def kernel(queries, passages, cand_rows, out, held, held_rows, own_for, corpus, rows_v, rows_s, score_out,
           score_in, own_rows, load_sem, in_sem, rows_sem, q_send, q_recv, r_send, r_recv, s_send, s_recv,
           ready_z, ready_y):
    me = lax.axis_index("shard")
    z, y = me // NY, me % NY
    bases = [plane(n, z) * NY for n in range(NZ)]
    others_y = [(y + dy) % NY for dy in range(1, NY)]

    def send(rows, s, to):
        for src, ref, send_sem, recv_sem in ((rows, held_rows, r_send, r_recv), (held.at[s], held, q_send, q_recv)):
            pltpu.make_async_remote_copy(
                src_ref=src, dst_ref=ref.at[s], send_sem=send_sem, recv_sem=recv_sem.at[s],
                device_id={"shard": to}, device_id_type=MESH).start()

    def send_own(to):
        send(own_for.at[to // NY], me, to)

    def wait_rows(s):
        pltpu.make_async_copy(held_rows.at[s], held_rows.at[s], r_recv.at[s]).wait()

    def wait_block(s):
        pltpu.make_async_copy(held.at[s], held.at[s], q_recv.at[s]).wait()

    def send_score(s):
        pltpu.make_async_remote_copy(
            src_ref=score_out.at[s], dst_ref=score_in.at[me], send_sem=s_send, recv_sem=s_recv,
            device_id={"shard": s}, device_id_type=MESH).start()

    def spread(i):
        s = bases[i] + y
        wait_rows(s)
        wait_block(s)
        for dy in (2, 1, 3):
            send(held_rows.at[s], s, z * NY + others_y[dy - 1])

    def member(i, j):
        return jnp.where(y == j, choose(bases[1:] + bases[-1:], i), choose(bases, i)) + j

    def unpack_rows(i):
        base = bases[i] if isinstance(i, int) else choose(bases, i)
        for other in others_y:
            wait_rows(base + other)
        mine = lax.broadcasted_iota(jnp.int32, (16, LANES), 0) == y
        for j in range(NY):
            rows = held_rows[member(i, j)].astype(jnp.float32)
            rows_v[i, j : j + 1] = jnp.sum(jnp.where(mine, rows, 0.0), axis=0, keepdims=True).astype(jnp.int32)
        pltpu.make_async_copy(rows_v.at[i], rows_s.at[i], rows_sem.at[i]).start()

    rows_in = pltpu.make_async_copy(cand_rows, own_rows, in_sem.at[0])
    queries_in = pltpu.make_async_copy(queries, held.at[me], in_sem.at[1])
    rows_in.start()
    queries_in.start()
    barrier = pltpu.get_barrier_semaphore()
    for d in range(1, NZ):
        to = (z + d) % NZ

        @pl.when(to > z)
        def _():
            pl.semaphore_signal(barrier, inc=1, device_id={"shard": to * NY + y}, device_id_type=MESH)

    for d in range(1, NY):
        to = (y + d) % NY

        @pl.when(to > y)
        def _():
            pl.semaphore_signal(barrier, inc=1, device_id={"shard": z * NY + to}, device_id_type=MESH)

    loads = []
    part = passages.shape[0] // 4
    for k in range(4):
        span = pl.ds(k * part, part)
        loads.append(pltpu.make_async_copy(passages.at[span], corpus.at[span], load_sem.at[k]))
        loads[-1].start()

    @pl.when(me > 0)
    def _():
        pl.semaphore_wait(barrier, z + y)

    for to in range(NY):

        @pl.when(to < y)
        def _():
            pl.semaphore_signal(ready_y.at[y], inc=1, device_id={"shard": z * NY + to}, device_id_type=MESH)

    for to in range(NZ):

        @pl.when(to < z)
        def _():
            pl.semaphore_signal(ready_z.at[z], inc=1, device_id={"shard": to * NY + y}, device_id_type=MESH)

    rows_in.wait()
    packed = jnp.concatenate([own_rows[q] for q in range(4)], axis=1).astype(jnp.float32)
    for to in range(NZ):
        piece = jnp.concatenate([packed[to * NY : (to + 1) * NY], jnp.zeros((16 - NY, LANES), jnp.float32)], axis=0)
        own_for[to] = piece.astype(jnp.bfloat16)
    held_rows[me] = own_for[z]
    queries_in.wait()

    for d in (1, 3, 2):
        to = apart(y, d)

        @pl.when(to < y)
        def _():
            send_own(z * NY + to)

    for k in (1, 2, 3):
        to = z - z % HALF + apart(z % HALF, k)

        @pl.when(to < z)
        def _():
            send_own(to * NY + y)

    def send_y(d):
        to = apart(y, d)

        @pl.when(to > y)
        def _():
            pl.semaphore_wait(ready_y.at[to], 1)
            send_own(z * NY + to)

    def send_z(other, k):
        to = HALF * ((z // HALF + other) % 2) + apart(z % HALF, k)

        @pl.when(to > z)
        def _():
            pl.semaphore_wait(ready_z.at[to], 1)
            send_own(to * NY + y)

        if other:

            @pl.when(to < z)
            def _():
                send_own(to * NY + y)

    def send_at(at):
        for here in range(NZ):
            if at in SENDS[here]:

                @pl.when(z == here)
                def _(here=here):
                    for kind, what in SENDS[here][at]:
                        if kind == "y":
                            send_y(what)
                        elif kind == "o":
                            send_z(*what)
                        else:
                            spread(what)

    mine = lax.broadcasted_iota(jnp.int32, (16, LANES), 0) == y
    own_row = jnp.sum(jnp.where(mine, held_rows[me].astype(jnp.float32), 0.0), axis=0, keepdims=True)
    rows_v[NZ] = jnp.broadcast_to(own_row.astype(jnp.int32), (NY, LANES))
    own_in = pltpu.make_async_copy(rows_v.at[NZ], rows_s.at[NZ], rows_sem.at[NZ])
    own_in.start()
    for load in loads:
        load.wait()
    own_in.wait()
    score_out[me] = score_block(held[me], lambda k: rows_s[NZ, 0, k], corpus)
    send_at(-1)
    unpack_rows(0)

    def early(i):
        low, high = (sum((i == k).astype(jnp.int32) for k in range(1, NZ) if at[k] < k) for at in ROWS_AT)
        return jnp.where(z < HALF, low, high) == 1

    def step(i, _):
        @pl.when(i > 0)
        def _():
            for j in range(NY):
                send_score(member(i - 1, j))

        for at in range(NZ):
            if any(at in SENDS[here] for here in range(NZ)):

                @pl.when(i == at)
                def _(at=at):
                    send_at(at)

        @pl.when((i > 0) & jnp.logical_not(early(i)))
        def _():
            unpack_rows(i)

        @pl.when(early(i + 1))
        def _():
            unpack_rows(i + 1)

        await_others(choose(bases, i))
        pltpu.make_async_copy(rows_v.at[i], rows_s.at[i], rows_sem.at[i]).wait()
        shards = [member(i, j) for j in range(NY)]
        for j, s in enumerate(shards):
            score_out[s] = score_block(held[s], lambda k, j=j: rows_s[i, j, k], corpus)
        return 0

    def await_others(base):
        for other in others_y:
            wait_block(base + other)

    last = NZ - 1
    lax.fori_loop(0, last, step, 0)
    for j in range(NY):
        send_score(member(last - 1, j))
    await_others(bases[last])
    pltpu.make_async_copy(rows_v.at[last], rows_s.at[last], rows_sem.at[last]).wait()
    for other in others_y:
        s = bases[last] + other
        score_out[s] = score_block(held[s], lambda k, other=other: rows_s[last, other, k], corpus)
    for other in others_y:
        send_score(bases[last] + other)
    others = pl.ds(0, N - 1)
    pltpu.make_async_copy(score_in.at[others], score_in.at[others], s_recv).wait()
    score_in[me] = score_out[me]
    returned = score_in[...].reshape(N, LANES)
    for q in range(4):
        out[q] = returned[:, q * CAP : (q + 1) * CAP]
    pltpu.make_async_copy(held.at[others], held.at[others], q_send).wait()
    pltpu.make_async_copy(held_rows.at[others], held_rows.at[others], r_send).wait()
    pltpu.make_async_copy(score_in.at[others], score_in.at[others], s_send).wait()


def body(queries, passages, cand_rows, cand_counts):
    count = queries.shape[0]
    block = queries.reshape(count * QTOK, queries.shape[2])
    hbm = pl.BlockSpec(memory_space=pltpu.HBM)
    dma = pltpu.SemaphoreType.DMA
    regular = pltpu.SemaphoreType.REGULAR
    returned = pl.pallas_call(
        kernel,
        out_shape=jax.ShapeDtypeStruct((count, N, CAP), jnp.float32),
        in_specs=[hbm, hbm, hbm],
        out_specs=pl.BlockSpec(memory_space=pltpu.VMEM),
        scratch_shapes=[
            pltpu.VMEM((N,) + block.shape, jnp.bfloat16),
            pltpu.VMEM((N, 16, LANES), jnp.bfloat16),
            pltpu.VMEM((NZ, 16, LANES), jnp.bfloat16),
            pltpu.VMEM(passages.shape, jnp.bfloat16),
            pltpu.VMEM((NZ + 1, NY, LANES), jnp.int32),
            pltpu.SMEM((NZ + 1, NY, LANES), jnp.int32),
            pltpu.VMEM((N, 1, LANES), jnp.float32),
            pltpu.VMEM((N, 1, LANES), jnp.float32),
            pltpu.VMEM(cand_rows.shape, jnp.int32),
            dma((4,)), dma((2,)), dma((NZ + 1,)),
            dma, dma((N,)), dma, dma((N,)), dma, dma,
            regular((NZ,)), regular((NY,)),
        ],
        compiler_params=pltpu.CompilerParams(collective_id=0, has_side_effects=True, vmem_limit_bytes=(64 << 20) - (64 << 10)),
        cost_estimate=pl.CostEstimate(flops=2 * 4096 * 72 * 32 * 128, bytes_accessed=6 << 20, transcendentals=0),
        name="maxsim",
    )(block, passages, cand_rows)
    live = jnp.arange(CAP)[None, None, :] < cand_counts[:, :, None]
    return jnp.where(live, returned, jnp.float32(0.0))


def solution(mesh):
    return jax.shard_map(
        body,
        mesh=mesh,
        in_specs=(
            P(("shard", "rep"), None, None),
            P("shard", None, None),
            P(("shard", "rep"), None, None),
            P(("shard", "rep"), None),
        ),
        out_specs=P(("shard", "rep"), None, None),
        check_vma=False,
    )
```
